128 devices in a mesh: group: 64 (over z, y, x), kv: 2 (over core).
Axes of the slice: x: 4, y: 4, z: 4, core: 2. Of those that a mesh axis runs over, the one named last changes fastest.
Arguments:
- lengths: int32 [64], P('group'), may hold values from 2048 to 8192, as said below
- latents: bfloat16 [64, 8192, 160], P('group', 'kv'), may hold values from -6 to 6
- codes: bfloat16 [64, 8192, 1024], P('group', 'kv'), may hold values from -10 to 10
- scales: bfloat16 [64, 32, 8], P('group', 'kv'), may hold values from 0.5 to 4
- queries: bfloat16 [64, 8, 8192], P('group'), may hold values from -900 to 900
- new_keys: bfloat16 [64, 8, 1024], P('group'), may hold values from -8 to 8
- new_values: bfloat16 [64, 8, 1024], P('group'), may hold values from -12 to 12
- key_factor: bfloat16 [160, 1024], replicated, may hold values from -0.5 to 0.5
- out_weight: bfloat16 [8192, 8192], P('kv', 'group'), may hold values from -0.0625 to 0.0625
Outputs:
- layer_out: float32 [512, 8192], P('kv', 'group')
The draws below stay inside these ranges and needn't reach their ends.
Inputs may be any that keep to these rules, and one draw needn't show every extreme that they name: `lengths`: one request has exactly 8192 cached tokens and one exactly 2048.
All inputs are finite; a program needn't handle non-finite values.
Results may differ from the reference program's by a relative error of at most 0.0087.
Values may be sent and summed in bfloat16 or wider, within the bound.
No kernel may reach another device: no remote copies, remote signals or barrier semaphores. Data moves between devices by JAX's collectives and lax.ppermute only.
A program may use at most 128 MiB of HBM per device.

```python
import math
import jax
import jax.numpy as jnp
from jax import lax

D = 8192
HEADS = 64
KV_HEADS = 8
HEAD_DIM = 128
RANK = 160
BLK = 256
Q_TOK = 8
REQS = 64
CTX = 8192


def drawn_base(key):
    return jax.random.normal(key, (REQS, Q_TOK, KV_HEADS, 1, HEAD_DIM), jnp.float32)


def draw_lengths(key, part):
    key = jax.random.fold_in(key, 11)
    key_tier, key_fill, key_top, key_low = jax.random.split(key, 4)
    tier_pick = jax.random.randint(key_tier, (REQS,), 0, 3)
    lowest = jnp.where(tier_pick == 2, CTX // 2, CTX // 4)
    spread = jnp.where(tier_pick == 2, CTX - CTX // 2, CTX // 2 - CTX // 4)
    drawn = lowest + jax.random.randint(key_fill, (REQS,), 0, 1 << 24) % spread
    top_index = jax.random.randint(key_top, (), 0, REQS)
    low_index = (top_index + 1 + jax.random.randint(key_low, (), 0, REQS - 1)) % REQS
    drawn = drawn.at[top_index].set(CTX).at[low_index].set(CTX // 4)
    return drawn.astype(jnp.int32)


def draw_codes(key, part):
    key = jax.random.fold_in(key, 23)
    key_centre, key_noise = jax.random.split(key)
    centre = jax.random.normal(key_centre, (REQS, 1, KV_HEADS * HEAD_DIM), jnp.float32)
    noise = jax.random.normal(key_noise, (REQS, CTX, KV_HEADS * HEAD_DIM), jnp.float32)
    return jnp.clip(centre + noise, -10.0, 10.0).astype(jnp.bfloat16)


def draw_queries(key, part):
    common = drawn_base(key)
    key = jax.random.fold_in(key, 31)
    key_noise = jax.random.fold_in(key, 0)
    noise = jax.random.normal(key_noise, (REQS, Q_TOK, KV_HEADS, HEADS // KV_HEADS, HEAD_DIM), jnp.float32)
    drawn = 1.05 * (common + noise)
    return jnp.clip(drawn, -900.0, 900.0).reshape(REQS, Q_TOK, HEADS * HEAD_DIM).astype(jnp.bfloat16)


def draw_new_keys(key, part):
    common = drawn_base(key)[:, :, :, 0, :]
    key = jax.random.fold_in(key, 37)
    noise = jax.random.normal(key, (REQS, Q_TOK, KV_HEADS, HEAD_DIM), jnp.float32)
    drawn = 0.7 * common + 0.3 * noise
    return jnp.clip(drawn, -8.0, 8.0).reshape(REQS, Q_TOK, KV_HEADS * HEAD_DIM).astype(jnp.bfloat16)


def block_levels(stream_key, dims, cuts, least, largest):
    gain, own = 1.0, jax.random.fold_in(stream_key, 6)
    for axis_at, parts in cuts:
        draws = jnp.exp(jax.random.uniform(jax.random.fold_in(own, axis_at), (parts,), jnp.float32, least / len(cuts), largest / len(cuts)))
        gain = gain * jnp.repeat(draws, dims[axis_at] // parts).reshape([-1 if axis == axis_at else 1 for axis in range(len(dims))])
    return gain


def normal_values(own_key, extent, deviation, bound, shards=(), kind=jnp.bfloat16):
    values = deviation * jax.random.normal(own_key, extent, jnp.float32)
    if shards:
        values = values * block_levels(own_key, extent, shards, -0.22, 0.18)
    return jnp.clip(values, -bound, bound).astype(kind)


def setup_inputs(seed: int = 0) -> dict:
    keys = jax.random.split(jax.random.key(seed), 10)
    lengths = draw_lengths(jax.random.fold_in(keys[9], 71), 0)
    latents = normal_values(keys[1], (REQS, CTX, RANK), 1.0, 6.0, ((0, 64), (1, 2)))
    codes = draw_codes(jax.random.fold_in(keys[9], 71), 0)
    scales = jnp.clip(jnp.exp(math.log(4.0) - 2.0794415 * jax.random.uniform(keys[3], (REQS, CTX // BLK, KV_HEADS), jnp.float32) ** block_levels(keys[3], (REQS, CTX // BLK, KV_HEADS), ((0, 64), (1, 2)), -0.2, 0.2)), 0.5, 4.0).astype(jnp.bfloat16)
    queries = draw_queries(jax.random.fold_in(keys[9], 71), 0)
    new_keys = draw_new_keys(jax.random.fold_in(keys[9], 71), 0)
    new_values = normal_values(keys[6], (REQS, Q_TOK, KV_HEADS * HEAD_DIM), 2.0, 12.0, ((0, 64),))
    key_factor = normal_values(keys[7], (RANK, KV_HEADS * HEAD_DIM), RANK ** -0.5, 0.5)
    out_weight = normal_values(keys[8], (HEADS * HEAD_DIM, D), (HEADS * HEAD_DIM) ** -0.5, 0.0625, ((0, 2), (1, 64)))
    return dict(lengths=lengths, latents=latents, codes=codes, scales=scales, queries=queries, new_keys=new_keys, new_values=new_values, key_factor=key_factor, out_weight=out_weight)


ROPE_BASE = 500000.0
NEG_FILL = -1.0e30


def rotate(key_before_rotary, positions):
    half_dim = HEAD_DIM // 2
    frequency = ROPE_BASE ** (-(jnp.arange(half_dim, dtype=jnp.float32) * 2.0) / HEAD_DIM)
    angles = positions.astype(jnp.float32)[:, None] * frequency[None, :]
    cosine = jnp.cos(angles)[:, None, :]
    sine_val = jnp.sin(angles)[:, None, :]
    lower_half = key_before_rotary[..., :half_dim]
    upper_half = key_before_rotary[..., half_dim:]
    return jnp.concatenate([lower_half * cosine - upper_half * sine_val, upper_half * cosine + lower_half * sine_val], axis=-1)


def reference(lengths, latents, codes, scales, queries, new_keys, new_values, key_factor, out_weight):
    groups = HEADS // KV_HEADS
    score_scale = HEAD_DIM ** -0.5

    def single_request(request_item):
        latent, code_rows, scale_rows, query_matrix_rows, fresh_keys, fresh_values, length = request_item
        key_before_rotary = jnp.dot(latent, key_factor, preferred_element_type=jnp.float32).reshape(CTX, KV_HEADS, HEAD_DIM)
        rotary_applied = rotate(key_before_rotary, jnp.arange(CTX, dtype=jnp.int32)).astype(jnp.bfloat16)
        rotary_applied = lax.optimization_barrier(rotary_applied).astype(jnp.float32)
        query_f = query_matrix_rows.astype(jnp.float32).reshape(Q_TOK, KV_HEADS, groups, HEAD_DIM)
        cache_scores = jnp.einsum('tkgd,ckd->tkgc', query_f, rotary_applied) * score_scale
        valid_mask = (jnp.arange(CTX, dtype=jnp.int32) < length)[None, None, None, :]
        cache_scores = jnp.where(valid_mask, cache_scores, NEG_FILL)
        fresh_f = fresh_keys.astype(jnp.float32).reshape(Q_TOK, KV_HEADS, HEAD_DIM)
        fresh_scores = jnp.einsum('tkgd,ukd->tkgu', query_f, fresh_f) * score_scale
        order_mask = jnp.arange(Q_TOK)[None, :] <= jnp.arange(Q_TOK)[:, None]
        causal = order_mask[:, None, None, :]
        fresh_scores = jnp.where(causal, fresh_scores, NEG_FILL)
        peak_score = jnp.maximum(jnp.max(cache_scores, axis=-1), jnp.max(fresh_scores, axis=-1))
        cache_weights = jnp.where(valid_mask, jnp.exp(cache_scores - peak_score[..., None]), 0.0)
        fresh_weights = jnp.where(causal, jnp.exp(fresh_scores - peak_score[..., None]), 0.0)
        totals = jnp.sum(cache_weights, axis=-1) + jnp.sum(fresh_weights, axis=-1)
        cache_rounded = lax.optimization_barrier(cache_weights.astype(jnp.bfloat16)).astype(jnp.float32)
        fresh_rounded = lax.optimization_barrier(fresh_weights.astype(jnp.bfloat16)).astype(jnp.float32)
        values = code_rows.astype(jnp.float32).reshape(CTX // BLK, BLK, KV_HEADS, HEAD_DIM)
        values = (values * scale_rows.astype(jnp.float32)[:, None, :, None]).reshape(CTX, KV_HEADS, HEAD_DIM)
        fresh_vals = fresh_values.astype(jnp.float32).reshape(Q_TOK, KV_HEADS, HEAD_DIM)
        numerator = jnp.einsum('tkgc,ckd->tkgd', cache_rounded, values) + jnp.einsum('tkgu,ukd->tkgd', fresh_rounded, fresh_vals)
        attended = numerator / totals[..., None]
        return attended.reshape(Q_TOK, HEADS * HEAD_DIM).astype(jnp.bfloat16)

    attended_all = lax.map(single_request, (latents, codes, scales, queries, new_keys, new_values, lengths))
    all_rows = attended_all.reshape(REQS * Q_TOK, HEADS * HEAD_DIM)
    return jnp.dot(all_rows, out_weight, preferred_element_type=jnp.float32)
```

```python
import functools

import jax
import jax.numpy as jnp
import numpy as np
from jax import lax
from jax.experimental import pallas as pl
from jax.experimental.pallas import tpu as pltpu
from jax.sharding import PartitionSpec as P

HEADS = 64
KV_HEADS = 8
HEAD_DIM = 128
HALF = HEAD_DIM // 2
RANK = 160
BLK = 256
CTX_DEV = 4096
Q_TOK = 8
PAIRS = KV_HEADS // 2
ROWS = 2 * (HEADS // KV_HEADS) * Q_TOK
CHUNK = 512
N_CHUNKS = CTX_DEV // CHUNK
ROPE_BASE = 500000.0
NEG_FILL = -1e30
EXP2_SCALE = float(HEAD_DIM**-0.5 * np.log2(np.e))


def rotary_tables():
    freq = np.float32(ROPE_BASE) ** (-(np.arange(HALF, dtype=np.float32) * 2.0) / HEAD_DIM)
    freq = np.tile(freq.astype(np.float32), 2).astype(np.float64)[None, :]
    inner = np.arange(BLK, dtype=np.float64)[:, None] * freq
    outer = np.arange(0, 2 * CTX_DEV, BLK, dtype=np.float64)[:, None] * freq
    return [f(a).astype(np.float32) for a in (inner, outer) for f in (np.cos, np.sin)]


def swap_halves(x):
    return pltpu.roll(x, HALF, 1)


def low_lanes(shape):
    return lax.broadcasted_iota(jnp.int32, shape, 1) < HALF


def pair_columns(even, odd):
    low = low_lanes(even.shape)
    return (
        jnp.where(low, even, swap_halves(odd)),
        jnp.where(low, swap_halves(even), odd),
    )


def attend_kernel(
    length_ref, lat_hbm, code_hbm, scale_ref, q_ref, nk_ref, nv_ref, kf_ref,
    cos_in, sin_in, cos_out, sin_out,
    mine_ref, send_ref,
    lat_buf, code_buf, lat_sem, code_sem, qc, wp, scale_rows, peak, total, numer,
):
    f32, bf16 = jnp.float32, jnp.bfloat16
    kv_at = lax.axis_index("kv")
    valid = jnp.clip(length_ref[0] - kv_at * CTX_DEV, 0, CTX_DEV)
    chunks = lax.div(valid + (CHUNK - 1), CHUNK)

    def copies(c):
        rows = pl.ds(pl.multiple_of(c * CHUNK, CHUNK), CHUNK)
        return (
            pltpu.make_async_copy(lat_hbm.at[rows], lat_buf.at[rows], lat_sem.at[c]),
            pltpu.make_async_copy(code_hbm.at[rows], code_buf.at[rows], code_sem.at[c]),
        )

    @pl.loop(0, chunks)
    def _(c):
        for copy in copies(c):
            copy.start()

    scales = scale_ref[...].astype(f32)
    for k in range(KV_HEADS):
        scale_rows[k] = jnp.broadcast_to(scales[:, k : k + 1], (CTX_DEV // BLK, HEAD_DIM))

    row_tok = lax.rem(lax.broadcasted_iota(jnp.int32, (ROWS, HEAD_DIM), 0), Q_TOK)
    lane = lax.broadcasted_iota(jnp.int32, (ROWS, HEAD_DIM), 1)
    causal = jnp.logical_and(lane <= row_tok, kv_at == 0)
    queries = q_ref[...].astype(f32)
    kf = kf_ref[...].astype(f32)
    new_keys = nk_ref[...].astype(f32)
    new_values = nv_ref[...].astype(f32)
    pad = jnp.zeros((HEAD_DIM - Q_TOK, 2 * HEAD_DIM), f32)

    def head_rows(k):
        groups = HEADS // KV_HEADS
        return jnp.concatenate(
            [queries[:, (k * groups + g) * HEAD_DIM : (k * groups + g + 1) * HEAD_DIM] for g in range(groups)],
            axis=0,
        )

    def two_heads(x, j):
        return (
            x[:, 2 * j * HEAD_DIM : (2 * j + 1) * HEAD_DIM],
            x[:, (2 * j + 1) * HEAD_DIM : (2 * j + 2) * HEAD_DIM],
        )

    def own_blocks(x):
        return jnp.concatenate([x[: ROWS // 2, :HEAD_DIM], x[ROWS // 2 :, HEAD_DIM:]], axis=0)

    def scores(a, b):
        return lax.dot_general(a, b, (((1,), (1,)), ((), ())), preferred_element_type=f32)

    for j in range(PAIRS):
        even, odd = head_rows(2 * j), head_rows(2 * j + 1)
        low = low_lanes(even.shape)
        qc[j] = jnp.concatenate(
            [
                jnp.concatenate(
                    [jnp.where(low, even, 0.0), jnp.where(low, swap_halves(even), 0.0)], axis=1
                ),
                jnp.concatenate(
                    [jnp.where(low, 0.0, swap_halves(odd)), jnp.where(low, 0.0, odd)], axis=1
                ),
            ],
            axis=0,
        ).astype(bf16)
        wp[:, 2 * j * HEAD_DIM : (2 * j + 2) * HEAD_DIM] = jnp.concatenate(
            pair_columns(*two_heads(kf, j)), axis=1
        ).astype(bf16)

        fresh_keys = jnp.concatenate(pair_columns(*two_heads(new_keys, j)), axis=1)
        fresh_keys = jnp.concatenate([fresh_keys, pad], axis=0).astype(bf16)
        fresh_values = jnp.concatenate(
            [new_values[:, 2 * j * HEAD_DIM : (2 * j + 2) * HEAD_DIM], pad], axis=0
        ).astype(bf16)
        s = jnp.where(causal, scores(qc[j], fresh_keys), NEG_FILL)
        top = jnp.broadcast_to(jnp.max(s, axis=1, keepdims=True), s.shape)
        weights = jnp.where(causal, jnp.exp2((s - top) * EXP2_SCALE), 0.0)
        peak[j] = top
        total[j] = weights
        numer[j] = own_blocks(
            jnp.dot(weights.astype(bf16), fresh_values, preferred_element_type=f32)
        )

    @pl.loop(0, chunks)
    def _(c):
        for copy in copies(c):
            copy.wait()
        rows = pl.ds(pl.multiple_of(c * CHUNK, CHUNK), CHUNK)
        lat = lat_buf[rows, :]
        cosines, sines = [], []
        for b in range(CHUNK // BLK):
            block = kv_at * (CTX_DEV // BLK) + c * (CHUNK // BLK) + b
            cos_b, sin_b = cos_out[pl.ds(block, 1), :], sin_out[pl.ds(block, 1), :]
            cosines.append(cos_in[...] * cos_b - sin_in[...] * sin_b)
            sines.append(sin_in[...] * cos_b + cos_in[...] * sin_b)
        cos, sin = jnp.concatenate(cosines, axis=0), jnp.concatenate(sines, axis=0)
        position = c * CHUNK + lax.broadcasted_iota(jnp.int32, (ROWS, CHUNK), 1)
        live = position < valid
        for j in range(PAIRS):
            columns = slice(2 * j * HEAD_DIM, (2 * j + 2) * HEAD_DIM)
            pre = jnp.dot(lat, wp[:, columns], preferred_element_type=f32)
            lo, hi = pre[:, :HEAD_DIM], pre[:, HEAD_DIM:]
            keys = jnp.concatenate(
                [(lo * cos - hi * sin).astype(bf16), (hi * cos + lo * sin).astype(bf16)], axis=1
            )
            s = jnp.where(live, scores(qc[j], keys), NEG_FILL)
            old = peak[j]
            new = jnp.maximum(old, jnp.max(s, axis=1, keepdims=True))
            shrink = jnp.exp2((old - new) * EXP2_SCALE)
            weights = [
                jnp.exp2((s[:, i : i + HEAD_DIM] - new) * EXP2_SCALE) for i in range(0, CHUNK, HEAD_DIM)
            ]
            peak[j] = new
            total[j] = total[j] * shrink + functools.reduce(jnp.add, weights)
            rounded = [w.astype(bf16) for w in weights]
            result = numer[j] * shrink
            for b in range(CHUNK // BLK):
                per = BLK // HEAD_DIM
                w = jnp.concatenate(rounded[b * per : (b + 1) * per], axis=1)
                v = code_buf[pl.ds(pl.multiple_of(c * CHUNK + b * BLK, BLK), BLK), columns]
                part = own_blocks(jnp.dot(w, v, preferred_element_type=f32))
                block = pl.ds(c * (CHUNK // BLK) + b, 1)
                factor = jnp.concatenate(
                    [
                        jnp.broadcast_to(scale_rows[2 * j + i, block, :], (ROWS // 2, HEAD_DIM))
                        for i in range(2)
                    ],
                    axis=0,
                )
                result = result + part * factor
            numer[j] = result

    for j in range(PAIRS):
        summed = jnp.broadcast_to(jnp.sum(total[j], axis=1, keepdims=True), (ROWS, HEAD_DIM))
        total[j] = jnp.where(low_lanes(summed.shape), peak[j], summed)
    half = PAIRS // 2
    for i in range(half):
        at = slice(i * ROWS, (i + 1) * ROWS)
        for ref, first in ((mine_ref, kv_at * half), (send_ref, (1 - kv_at) * half)):
            ref[at, :HEAD_DIM] = numer[first + i]
            ref[at, HEAD_DIM:] = total[first + i]


def attend(length, latents, codes, scales, queries, new_keys, new_values, key_factor):
    f32, bf16 = jnp.float32, jnp.bfloat16
    vmem = pl.BlockSpec(memory_space=pltpu.VMEM)
    hbm = pl.BlockSpec(memory_space=pl.ANY)
    shape = jax.ShapeDtypeStruct((PAIRS // 2 * ROWS, 2 * HEAD_DIM), f32)
    macs = CTX_DEV * (RANK * KV_HEADS + 2 * PAIRS * ROWS * 2) * HEAD_DIM
    return pl.pallas_call(
        attend_kernel,
        out_shape=(shape, shape),
        in_specs=[pl.BlockSpec(memory_space=pltpu.SMEM), hbm, hbm] + [vmem] * 9,
        out_specs=(vmem, vmem),
        scratch_shapes=[
            pltpu.VMEM((CTX_DEV, RANK), bf16),
            pltpu.VMEM((CTX_DEV, KV_HEADS * HEAD_DIM), bf16),
            pltpu.SemaphoreType.DMA((N_CHUNKS,)),
            pltpu.SemaphoreType.DMA((N_CHUNKS,)),
            pltpu.VMEM((PAIRS, ROWS, 2 * HEAD_DIM), bf16),
            pltpu.VMEM((RANK, KV_HEADS * HEAD_DIM), bf16),
            pltpu.VMEM((KV_HEADS, CTX_DEV // BLK, HEAD_DIM), f32),
            pltpu.VMEM((PAIRS, ROWS, HEAD_DIM), f32),
            pltpu.VMEM((PAIRS, ROWS, HEAD_DIM), f32),
            pltpu.VMEM((PAIRS, ROWS, HEAD_DIM), f32),
        ],
        compiler_params=pltpu.CompilerParams(vmem_limit_bytes=40 * 2**20),
        cost_estimate=pl.CostEstimate(
            flops=2 * macs, bytes_accessed=12 * 2**20, transcendentals=CTX_DEV * HEADS * Q_TOK
        ),
        name="attend",
    )(length, latents, codes, scales, queries, new_keys, new_values, key_factor,
      *[jnp.asarray(t) for t in rotary_tables()])


def merge_kernel(a_ref, b_ref, out_ref):
    def parts(ref):
        both = ref[:, HEAD_DIM:]
        low, other = low_lanes(both.shape), swap_halves(both)
        return ref[:, :HEAD_DIM], jnp.where(low, both, other), jnp.where(low, other, both)

    numer_a, peak_a, total_a = parts(a_ref)
    numer_b, peak_b, total_b = parts(b_ref)
    peak = jnp.maximum(peak_a, peak_b)
    weight_a = jnp.exp2((peak_a - peak) * EXP2_SCALE)
    weight_b = jnp.exp2((peak_b - peak) * EXP2_SCALE)
    out = (numer_a * weight_a + numer_b * weight_b) / (total_a * weight_a + total_b * weight_b)
    out_ref[...] = jnp.concatenate(
        [out[i : i + Q_TOK] for i in range(0, out.shape[0], Q_TOK)], axis=1
    ).astype(out_ref.dtype)


def merge(mine, other):
    vmem = pl.BlockSpec(memory_space=pltpu.VMEM)
    return pl.pallas_call(
        merge_kernel,
        out_shape=jax.ShapeDtypeStruct((Q_TOK, HEADS // 2 * HEAD_DIM), jnp.bfloat16),
        in_specs=[vmem, vmem],
        out_specs=vmem,
        name="merge",
    )(mine, other)


def other_core(x):
    return lax.ppermute(x, "kv", [(0, 1), (1, 0)])


def body(lengths, latents, codes, scales, queries, new_keys, new_values, key_factor, out_weight):
    kv_at = lax.axis_index("kv")
    mine, send = attend(
        lengths, latents[0], codes[0], scales[0], queries[0], new_keys[0], new_values[0], key_factor
    )
    attended = merge(mine, other_core(send))
    all_rows = lax.all_gather(attended, "group", axis=0, tiled=True)
    out = jnp.dot(all_rows, out_weight, preferred_element_type=jnp.float32)
    half = out.shape[0] // 2
    keep = lax.dynamic_slice_in_dim(out, kv_at * half, half, 0)
    give = lax.dynamic_slice_in_dim(out, (1 - kv_at) * half, half, 0)
    return keep + other_core(give)


def solution(mesh):
    placed = (
        P("group"),
        P("group", "kv", None),
        P("group", "kv", None),
        P("group", "kv", None),
        P("group", None, None),
        P("group", None, None),
        P("group", None, None),
        P(),
        P("kv", "group"),
    )
    return jax.shard_map(
        body, mesh=mesh, in_specs=placed, out_specs=P("kv", "group"), check_vma=False
    )
```

```python
import functools

import jax
import jax.numpy as jnp
import numpy as np
from jax import lax
from jax.experimental import pallas as pl
from jax.experimental.pallas import tpu as pltpu
from jax.sharding import PartitionSpec as P

HEADS = 64
KV_HEADS = 8
HEAD_DIM = 128
HALF = HEAD_DIM // 2
RANK = 160
BLK = 256
CTX_DEV = 4096
Q_TOK = 8
PAIRS = KV_HEADS // 2
ROWS = 2 * (HEADS // KV_HEADS) * Q_TOK
CHUNK = 2048
N_CHUNKS = CTX_DEV // CHUNK
ROPE_BASE = 500000.0
NEG_FILL = -1e30
EXP2_SCALE = float(HEAD_DIM**-0.5 * np.log2(np.e))


def rotary_table():
    freq = np.float32(ROPE_BASE) ** (-(np.arange(HALF, dtype=np.float32) * 2.0) / HEAD_DIM)
    angles = np.arange(2 * CTX_DEV, dtype=np.float32)[None, :] * freq.astype(np.float32)[:, None]
    angles = angles.reshape(HALF, 2, CTX_DEV).astype(np.float64)
    return np.stack([np.cos(angles), np.sin(angles)]).transpose(2, 0, 1, 3).astype(np.float32)


STRIP = 16


def strip_order():
    starts = [
        head * HEAD_DIM + half * HALF + m * STRIP
        for m in range(HALF // STRIP)
        for head in range(2)
        for half in range(2)
    ]
    return np.concatenate([np.arange(a, a + STRIP) for a in starts])


def swap_halves(x):
    return pltpu.roll(x, HALF, 1)


def low_lanes(shape):
    return lax.broadcasted_iota(jnp.int32, shape, 1) < HALF


def dot(a, b):
    return jnp.dot(a, b, preferred_element_type=jnp.float32)


def own_blocks(x):
    return jnp.concatenate([x[: ROWS // 2, :HEAD_DIM], x[ROWS // 2 :, HEAD_DIM:]], axis=0)


def attend_kernel(
    length_ref, lat_hbm, code_hbm, table_hbm, scale_hbm, q_hbm, nk_hbm, nv_hbm, kf_hbm,
    mine_ref, send_ref,
    lat_buf, code_buf, table_buf, scale_buf, q_buf, nk_buf, nv_buf, kf_buf,
    lat_sem, code_sem, table_sem, small_sem,
    qc, wt, scale_rows, peak, total, numer,
):
    f32, bf16 = jnp.float32, jnp.bfloat16
    kv_at = lax.axis_index("kv")
    valid = jnp.clip(length_ref[0] - kv_at * CTX_DEV, 0, CTX_DEV)
    chunks = lax.div(valid + (CHUNK - 1), CHUNK)

    small = [
        pltpu.make_async_copy(src, dst, small_sem.at[i])
        for i, (src, dst) in enumerate(
            ((kf_hbm, kf_buf), (q_hbm, q_buf), (nk_hbm, nk_buf), (nv_hbm, nv_buf), (scale_hbm, scale_buf))
        )
    ]
    for copy in small:
        copy.start()

    def copies(c):
        at = pl.ds(pl.multiple_of(c * CHUNK, CHUNK), CHUNK)
        return (
            pltpu.make_async_copy(lat_hbm.at[:, at], lat_buf.at[:, at], lat_sem.at[c]),
            pltpu.make_async_copy(table_hbm.at[kv_at, :, :, at], table_buf.at[:, :, at], table_sem.at[c]),
            pltpu.make_async_copy(code_hbm.at[at], code_buf.at[at], code_sem.at[c]),
        )

    @pl.loop(0, chunks)
    def _(c):
        for copy in copies(c):
            copy.start()

    for copy in small:
        copy.wait()
    scales = scale_buf[...].astype(f32)
    for b in range(CTX_DEV // BLK):
        scale_rows[b] = jnp.broadcast_to(scales[:, b : b + 1], (KV_HEADS, HEAD_DIM))
    row_tok = lax.rem(lax.broadcasted_iota(jnp.int32, (ROWS, HEAD_DIM), 0), Q_TOK)
    lane = lax.broadcasted_iota(jnp.int32, (ROWS, HEAD_DIM), 1)
    causal = jnp.logical_and(lane <= row_tok, kv_at == 0)
    queries = q_buf[...].astype(f32)
    new_keys = nk_buf[...].astype(f32)
    new_values = nv_buf[...].astype(f32)
    pad = jnp.zeros((HEAD_DIM - Q_TOK, 2 * HEAD_DIM), f32)
    groups = HEADS // KV_HEADS
    blank = jnp.zeros((ROWS // 2, HEAD_DIM), f32)

    def head_rows(k):
        return jnp.concatenate(
            [queries[:, (k * groups + g) * HEAD_DIM : (k * groups + g + 1) * HEAD_DIM] for g in range(groups)],
            axis=0,
        )

    order = strip_order()
    source = lax.broadcasted_iota(jnp.int32, (2 * HEAD_DIM, 2 * HEAD_DIM), 0)
    target = lax.broadcasted_iota(jnp.int32, (2 * HEAD_DIM, 2 * HEAD_DIM), 1)
    strip, inside = lax.div(target, STRIP), lax.rem(target, STRIP)
    wanted = (
        lax.rem(lax.div(strip, 2), 2) * HEAD_DIM + lax.rem(strip, 2) * HALF + lax.div(strip, 4) * STRIP + inside
    )
    arrange = jnp.where(source == wanted, 1.0, 0.0).astype(bf16)

    for j in range(PAIRS):
        columns = slice(2 * j * HEAD_DIM, (2 * j + 2) * HEAD_DIM)
        plain = jnp.concatenate(
            [
                jnp.concatenate([head_rows(2 * j), blank], axis=1),
                jnp.concatenate([blank, head_rows(2 * j + 1)], axis=1),
            ],
            axis=0,
        ).astype(bf16)
        qc[j] = dot(plain, arrange).astype(bf16)
        turned = kf_buf[:, columns].astype(f32).T
        wt[columns, :] = jnp.concatenate(
            [turned[a : a + STRIP] for a in order[::STRIP]], axis=0
        ).astype(bf16)
        fresh_keys = jnp.concatenate([new_keys[:, columns], pad], axis=0).astype(bf16)
        fresh_values = jnp.concatenate([new_values[:, columns], pad], axis=0).astype(bf16)
        s = lax.dot_general(plain, fresh_keys, (((1,), (1,)), ((), ())), preferred_element_type=f32)
        s = jnp.where(causal, s, NEG_FILL)
        top = jnp.broadcast_to(jnp.max(s, axis=1, keepdims=True), s.shape)
        weights = jnp.where(causal, jnp.exp2((s - top) * EXP2_SCALE), 0.0)
        peak[j] = top
        total[j] = weights
        numer[j] = own_blocks(dot(weights.astype(bf16), fresh_values))

    @pl.loop(0, chunks)
    def _(c):
        for copy in copies(c):
            copy.wait()
        at = pl.ds(pl.multiple_of(c * CHUNK, CHUNK), CHUNK)
        lat = lat_buf[:, at]
        position = c * CHUNK + lax.broadcasted_iota(jnp.int32, (1, CHUNK), 1)
        hide = jnp.where(position < valid, 0.0, NEG_FILL)
        def make_keys(j):
            columns = slice(2 * j * HEAD_DIM, (2 * j + 2) * HEAD_DIM)
            cos, sin = table_buf[0, :, at], table_buf[1, :, at]
            pre = dot(wt[columns, :], lat)
            keys = []
            for m in range(HALF // STRIP):
                here = slice(m * STRIP, (m + 1) * STRIP)
                for i in range(2):
                    at_lo = (4 * m + 2 * i) * STRIP
                    lo, hi = pre[at_lo : at_lo + STRIP], pre[at_lo + STRIP : at_lo + 2 * STRIP]
                    keys.append((lo * cos[here] - hi * sin[here]).astype(bf16))
                    keys.append((hi * cos[here] + lo * sin[here]).astype(bf16))
            return jnp.concatenate(keys, axis=0)

        def make_scores(j, keys):
            return dot(qc[j], keys) + hide

        def weigh(j, s):
            old = peak[j]
            new = jnp.maximum(old, jnp.max(s, axis=1, keepdims=True))
            shrink = jnp.exp2((old - new) * EXP2_SCALE)
            weights = [
                jnp.exp2((s[:, i : i + HEAD_DIM] - new) * EXP2_SCALE) for i in range(0, CHUNK, HEAD_DIM)
            ]
            peak[j] = new
            total[j] = total[j] * shrink + functools.reduce(jnp.add, weights)
            return shrink, [w.astype(bf16) for w in weights]

        def add_values(j, shrink, rounded):
            columns = slice(2 * j * HEAD_DIM, (2 * j + 2) * HEAD_DIM)
            result = numer[j] * shrink
            for b in range(CHUNK // BLK):
                per = BLK // HEAD_DIM
                w = jnp.concatenate(rounded[b * per : (b + 1) * per], axis=1)
                v = code_buf[pl.ds(pl.multiple_of(c * CHUNK + b * BLK, BLK), BLK), columns]
                part = own_blocks(dot(w, v))
                block = c * (CHUNK // BLK) + b
                factor = jnp.concatenate(
                    [
                        jnp.broadcast_to(scale_rows[block, 2 * j + i : 2 * j + i + 1, :], (ROWS // 2, HEAD_DIM))
                        for i in range(2)
                    ],
                    axis=0,
                )
                result = result + part * factor
            numer[j] = result

        all_keys = [make_keys(j) for j in range(PAIRS)]
        all_scores = [make_scores(j, all_keys[j]) for j in range(PAIRS)]
        weighed = [weigh(j, all_scores[j]) for j in range(PAIRS)]
        for j in range(PAIRS):
            add_values(j, *weighed[j])

    for j in range(PAIRS):
        summed = jnp.broadcast_to(jnp.sum(total[j], axis=1, keepdims=True), (ROWS, HEAD_DIM))
        total[j] = jnp.where(low_lanes(summed.shape), peak[j], summed)
    half = PAIRS // 2
    for i in range(half):
        at = slice(i * ROWS, (i + 1) * ROWS)
        for ref, first in ((mine_ref, kv_at * half), (send_ref, (1 - kv_at) * half)):
            ref[at, :HEAD_DIM] = numer[first + i]
            ref[at, HEAD_DIM:] = total[first + i]


def attend(length, latents, codes, scales, queries, new_keys, new_values, key_factor):
    f32, bf16 = jnp.float32, jnp.bfloat16
    vmem = pl.BlockSpec(memory_space=pltpu.VMEM)
    hbm = pl.BlockSpec(memory_space=pltpu.HBM)
    shape = jax.ShapeDtypeStruct((PAIRS // 2 * ROWS, 2 * HEAD_DIM), f32)
    macs = CTX_DEV * (RANK * KV_HEADS + 2 * PAIRS * ROWS * 2) * HEAD_DIM
    width = KV_HEADS * HEAD_DIM
    return pl.pallas_call(
        attend_kernel,
        out_shape=(shape, shape),
        in_specs=[pl.BlockSpec(memory_space=pltpu.SMEM)] + [hbm] * 8,
        out_specs=(vmem, vmem),
        scratch_shapes=[
            pltpu.VMEM((RANK, CTX_DEV), bf16),
            pltpu.VMEM((CTX_DEV, width), bf16),
            pltpu.VMEM((2, HALF, CTX_DEV), f32),
            pltpu.VMEM((KV_HEADS, CTX_DEV // BLK), bf16),
            pltpu.VMEM((Q_TOK, HEADS * HEAD_DIM), bf16),
            pltpu.VMEM((Q_TOK, width), bf16),
            pltpu.VMEM((Q_TOK, width), bf16),
            pltpu.VMEM((RANK, width), bf16),
            pltpu.SemaphoreType.DMA((N_CHUNKS,)),
            pltpu.SemaphoreType.DMA((N_CHUNKS,)),
            pltpu.SemaphoreType.DMA((N_CHUNKS,)),
            pltpu.SemaphoreType.DMA((5,)),
            pltpu.VMEM((PAIRS, ROWS, 2 * HEAD_DIM), bf16),
            pltpu.VMEM((width, RANK), bf16),
            pltpu.VMEM((CTX_DEV // BLK, KV_HEADS, HEAD_DIM), f32),
            pltpu.VMEM((PAIRS, ROWS, HEAD_DIM), f32),
            pltpu.VMEM((PAIRS, ROWS, HEAD_DIM), f32),
            pltpu.VMEM((PAIRS, ROWS, HEAD_DIM), f32),
        ],
        compiler_params=pltpu.CompilerParams(vmem_limit_bytes=60 * 2**20),
        cost_estimate=pl.CostEstimate(
            flops=2 * macs, bytes_accessed=12 * 2**20, transcendentals=CTX_DEV * HEADS * Q_TOK
        ),
        name="attend",
    )(length, latents.T, codes, jnp.asarray(rotary_table()), scales.T, queries, new_keys, new_values, key_factor)


def merge_kernel(a_ref, b_ref, out_ref):
    def parts(ref):
        both = ref[:, HEAD_DIM:]
        low, other = low_lanes(both.shape), swap_halves(both)
        return ref[:, :HEAD_DIM], jnp.where(low, both, other), jnp.where(low, other, both)

    numer_a, peak_a, total_a = parts(a_ref)
    numer_b, peak_b, total_b = parts(b_ref)
    peak = jnp.maximum(peak_a, peak_b)
    weight_a = jnp.exp2((peak_a - peak) * EXP2_SCALE)
    weight_b = jnp.exp2((peak_b - peak) * EXP2_SCALE)
    out = (numer_a * weight_a + numer_b * weight_b) / (total_a * weight_a + total_b * weight_b)
    out_ref[...] = jnp.concatenate(
        [out[i : i + Q_TOK] for i in range(0, out.shape[0], Q_TOK)], axis=1
    ).astype(out_ref.dtype)


def merge(mine, other):
    vmem = pl.BlockSpec(memory_space=pltpu.VMEM)
    return pl.pallas_call(
        merge_kernel,
        out_shape=jax.ShapeDtypeStruct((Q_TOK, HEADS // 2 * HEAD_DIM), jnp.bfloat16),
        in_specs=[vmem, vmem],
        out_specs=vmem,
        name="merge",
    )(mine, other)


def other_core(x):
    return lax.ppermute(x, "kv", [(0, 1), (1, 0)])


AXES = {"z": 16, "y": 4, "x": 1}
SIDE = 4
WEIGHT_AXIS = ("x", "y")
FIRST_AXIS = ("y", "z")
SECOND_AXIS = ("z", "x")
SHIFTS = (1, -1, 2)


def coordinate(chip, axis):
    return chip // AXES[axis] % SIDE


def shifted(x, axes, shift):
    moves = []
    for chip in range(SIDE**3):
        for core, axis in enumerate(axes):
            at = coordinate(chip, axis)
            target = chip + ((at + shift) % SIDE - at) * AXES[axis]
            moves.append((chip * 2 + core, target * 2 + core))
    return lax.ppermute(x, ("group", "kv"), moves)


def gathered(x, axes):
    return jnp.concatenate([x] + [shifted(x, axes, shift) for shift in SHIFTS], axis=0)


def assemble_kernel(p0_ref, p1_ref, p2_ref, p3_ref, keep_ref, give_ref, whole):
    chip, core = lax.axis_index("group"), lax.axis_index("kv")

    def axis_at(axes):
        return [lax.rem(lax.div(chip, AXES[axis]), SIDE) for axis in axes]

    def place(axes, core_at):
        return jnp.where(core_at == 0, *[jnp.int32(AXES[axis]) for axis in axes])

    weight, first, second = (
        jnp.where(core == 0, *axis_at(axes)) for axes in (WEIGHT_AXIS, FIRST_AXIS, SECOND_AXIS)
    )
    steps = (0,) + SHIFTS
    for ref, d in zip((p0_ref, p1_ref, p2_ref, p3_ref), steps):
        for i, e in enumerate(steps):
            for j, f in enumerate(steps):
                request = (
                    lax.rem(weight + (d + SIDE), SIDE) * place(WEIGHT_AXIS, core)
                    + lax.rem(first + (SIDE - f), SIDE) * place(FIRST_AXIS, core)
                    + lax.rem(second + (SIDE - e), SIDE) * place(SECOND_AXIS, core)
                )
                row = (i * SIDE + j) * Q_TOK
                whole[pl.ds(pl.multiple_of(request * Q_TOK, Q_TOK), Q_TOK), :] = ref[row : row + Q_TOK, :]
    half = whole.shape[0] // 2
    keep_ref[...] = whole[pl.ds(pl.multiple_of(core * half, half), half), :]
    give_ref[...] = whole[pl.ds(pl.multiple_of((1 - core) * half, half), half), :]


def assemble(pieces):
    vmem = pl.BlockSpec(memory_space=pltpu.VMEM)
    rows, columns = SIDE * pieces[0].shape[0], pieces[0].shape[1]
    shape = jax.ShapeDtypeStruct((rows // 2, columns), jnp.float32)
    return pl.pallas_call(
        assemble_kernel,
        out_shape=(shape, shape),
        in_specs=[vmem] * 4,
        out_specs=(vmem, vmem),
        scratch_shapes=[pltpu.VMEM((rows, columns), jnp.float32)],
        name="assemble",
    )(*pieces)


def body(lengths, latents, codes, scales, queries, new_keys, new_values, key_factor, out_weight):
    weights = [out_weight] + [shifted(out_weight, WEIGHT_AXIS, shift) for shift in SHIFTS]
    mine, send = attend(
        lengths, latents[0], codes[0], scales[0], queries[0], new_keys[0], new_values[0], key_factor
    )
    attended = merge(mine, other_core(send))
    rows = gathered(gathered(attended, FIRST_AXIS), SECOND_AXIS)
    results = [dot(rows, w) for w in weights]
    pieces = [results[0]] + [shifted(r, WEIGHT_AXIS, -shift) for r, shift in zip(results[1:], SHIFTS)]
    keep, give = assemble(pieces)
    return keep + other_core(give)


def solution(mesh):
    placed = (
        P("group"),
        P("group", "kv", None),
        P("group", "kv", None),
        P("group", "kv", None),
        P("group", None, None),
        P("group", None, None),
        P("group", None, None),
        P(),
        P("kv", "group"),
    )
    return jax.shard_map(
        body, mesh=mesh, in_specs=placed, out_specs=P("kv", "group"), check_vma=False
    )
```

```python
import functools

import jax
import jax.numpy as jnp
import numpy as np
from jax import lax
from jax.experimental import pallas as pl
from jax.experimental.pallas import tpu as pltpu
from jax.sharding import PartitionSpec as P

HEADS = 64
KV_HEADS = 8
HEAD_DIM = 128
HALF = HEAD_DIM // 2
RANK = 160
BLK = 256
CTX_DEV = 4096
Q_TOK = 8
PAIRS = KV_HEADS // 2
ROWS = 2 * (HEADS // KV_HEADS) * Q_TOK
CHUNK = 2048
N_CHUNKS = CTX_DEV // CHUNK
ROPE_BASE = 500000.0
NEG_FILL = -1e30
EXP2_SCALE = float(HEAD_DIM**-0.5 * np.log2(np.e))


def rotary_table():
    freq = np.float32(ROPE_BASE) ** (-(np.arange(HALF, dtype=np.float32) * 2.0) / HEAD_DIM)
    angles = np.arange(2 * CTX_DEV, dtype=np.float32)[None, :] * freq.astype(np.float32)[:, None]
    angles = angles.reshape(HALF, 2, CTX_DEV).astype(np.float64)
    return np.stack([np.cos(angles), np.sin(angles)]).transpose(2, 0, 1, 3).astype(np.float32)


STRIP = 16


def strip_order():
    starts = [
        head * HEAD_DIM + half * HALF + m * STRIP
        for m in range(HALF // STRIP)
        for head in range(2)
        for half in range(2)
    ]
    return np.concatenate([np.arange(a, a + STRIP) for a in starts])


def dot(a, b):
    return jnp.dot(a, b, preferred_element_type=jnp.float32)


def own_blocks(x):
    return jnp.concatenate([x[: ROWS // 2, :HEAD_DIM], x[ROWS // 2 :, HEAD_DIM:]], axis=0)


def attend_kernel(
    length_ref, lat_hbm, code_hbm, table_hbm, scale_hbm, q_hbm, nk_hbm, nv_hbm, kf_hbm,
    mine_ref, send_ref,
    lat_buf, code_buf, table_buf, scale_buf, q_buf, nk_buf, nv_buf, kf_buf,
    lat_sem, code_sem, table_sem, small_sem,
    qc, wt, scale_rows, peak, total, numer,
):
    f32, bf16 = jnp.float32, jnp.bfloat16
    kv_at = lax.axis_index("kv")
    valid = jnp.clip(length_ref[0] - kv_at * CTX_DEV, 0, CTX_DEV)
    chunks = lax.div(valid + (CHUNK - 1), CHUNK)

    small = [
        pltpu.make_async_copy(src, dst, small_sem.at[i])
        for i, (src, dst) in enumerate(
            ((kf_hbm, kf_buf), (q_hbm, q_buf), (nk_hbm, nk_buf), (nv_hbm, nv_buf), (scale_hbm, scale_buf))
        )
    ]
    for copy in small:
        copy.start()

    def copies(c):
        at = pl.ds(pl.multiple_of(c * CHUNK, CHUNK), CHUNK)
        return (
            pltpu.make_async_copy(lat_hbm.at[:, at], lat_buf.at[:, at], lat_sem.at[c]),
            pltpu.make_async_copy(table_hbm.at[kv_at, :, :, at], table_buf.at[:, :, at], table_sem.at[c]),
            pltpu.make_async_copy(code_hbm.at[at], code_buf.at[at], code_sem.at[c]),
        )

    @pl.loop(0, chunks)
    def _(c):
        for copy in copies(c):
            copy.start()

    for copy in small:
        copy.wait()
    scales = scale_buf[...].astype(f32)
    for b in range(CTX_DEV // BLK):
        scale_rows[b] = jnp.broadcast_to(scales[:, b : b + 1], (KV_HEADS, HEAD_DIM))
    row_tok = lax.rem(lax.broadcasted_iota(jnp.int32, (ROWS, HEAD_DIM), 0), Q_TOK)
    lane = lax.broadcasted_iota(jnp.int32, (ROWS, HEAD_DIM), 1)
    causal = jnp.logical_and(lane <= row_tok, kv_at == 0)
    queries = q_buf[...].astype(f32)
    new_keys = nk_buf[...].astype(f32)
    new_values = nv_buf[...].astype(f32)
    pad = jnp.zeros((HEAD_DIM - Q_TOK, 2 * HEAD_DIM), f32)
    groups = HEADS // KV_HEADS
    blank = jnp.zeros((ROWS // 2, HEAD_DIM), f32)

    def head_rows(k):
        return jnp.concatenate(
            [queries[:, (k * groups + g) * HEAD_DIM : (k * groups + g + 1) * HEAD_DIM] for g in range(groups)],
            axis=0,
        )

    order = strip_order()
    source = lax.broadcasted_iota(jnp.int32, (2 * HEAD_DIM, 2 * HEAD_DIM), 0)
    target = lax.broadcasted_iota(jnp.int32, (2 * HEAD_DIM, 2 * HEAD_DIM), 1)
    strip, inside = lax.div(target, STRIP), lax.rem(target, STRIP)
    wanted = (
        lax.rem(lax.div(strip, 2), 2) * HEAD_DIM + lax.rem(strip, 2) * HALF + lax.div(strip, 4) * STRIP + inside
    )
    arrange = jnp.where(source == wanted, 1.0, 0.0).astype(bf16)

    for j in range(PAIRS):
        columns = slice(2 * j * HEAD_DIM, (2 * j + 2) * HEAD_DIM)
        plain = jnp.concatenate(
            [
                jnp.concatenate([head_rows(2 * j), blank], axis=1),
                jnp.concatenate([blank, head_rows(2 * j + 1)], axis=1),
            ],
            axis=0,
        ).astype(bf16)
        qc[j] = dot(plain, arrange).astype(bf16)
        turned = kf_buf[:, columns].astype(f32).T
        wt[columns, :] = jnp.concatenate(
            [turned[a : a + STRIP] for a in order[::STRIP]], axis=0
        ).astype(bf16)
        fresh_keys = jnp.concatenate([new_keys[:, columns], pad], axis=0).astype(bf16)
        fresh_values = jnp.concatenate([new_values[:, columns], pad], axis=0).astype(bf16)
        s = lax.dot_general(plain, fresh_keys, (((1,), (1,)), ((), ())), preferred_element_type=f32)
        s = jnp.where(causal, s, NEG_FILL)
        top = jnp.broadcast_to(jnp.max(s, axis=1, keepdims=True), s.shape)
        weights = jnp.where(causal, jnp.exp2((s - top) * EXP2_SCALE), 0.0)
        peak[j] = top
        total[j] = weights
        numer[j] = own_blocks(dot(weights.astype(bf16), fresh_values))

    @pl.loop(0, chunks)
    def _(c):
        for copy in copies(c):
            copy.wait()
        at = pl.ds(pl.multiple_of(c * CHUNK, CHUNK), CHUNK)
        lat = lat_buf[:, at]
        position = c * CHUNK + lax.broadcasted_iota(jnp.int32, (1, CHUNK), 1)
        hide = jnp.where(position < valid, 0.0, NEG_FILL)
        def make_keys(j):
            columns = slice(2 * j * HEAD_DIM, (2 * j + 2) * HEAD_DIM)
            cos, sin = table_buf[0, :, at], table_buf[1, :, at]
            pre = dot(wt[columns, :], lat)
            keys = []
            for m in range(HALF // STRIP):
                here = slice(m * STRIP, (m + 1) * STRIP)
                for i in range(2):
                    at_lo = (4 * m + 2 * i) * STRIP
                    lo, hi = pre[at_lo : at_lo + STRIP], pre[at_lo + STRIP : at_lo + 2 * STRIP]
                    keys.append((lo * cos[here] - hi * sin[here]).astype(bf16))
                    keys.append((hi * cos[here] + lo * sin[here]).astype(bf16))
            return jnp.concatenate(keys, axis=0)

        def make_scores(j, keys):
            return dot(qc[j], keys) + hide

        def weigh(j, s):
            old = peak[j]
            new = jnp.maximum(old, jnp.max(s, axis=1, keepdims=True))
            shrink = jnp.exp2((old - new) * EXP2_SCALE)
            weights = [
                jnp.exp2((s[:, i : i + HEAD_DIM] - new) * EXP2_SCALE) for i in range(0, CHUNK, HEAD_DIM)
            ]
            peak[j] = new
            total[j] = total[j] * shrink + functools.reduce(jnp.add, weights)
            return shrink, [w.astype(bf16) for w in weights]

        def add_values(j, shrink, rounded):
            columns = slice(2 * j * HEAD_DIM, (2 * j + 2) * HEAD_DIM)
            result = numer[j] * shrink
            for b in range(CHUNK // BLK):
                per = BLK // HEAD_DIM
                w = jnp.concatenate(rounded[b * per : (b + 1) * per], axis=1)
                v = code_buf[pl.ds(pl.multiple_of(c * CHUNK + b * BLK, BLK), BLK), columns]
                part = own_blocks(dot(w, v))
                block = c * (CHUNK // BLK) + b
                factor = jnp.concatenate(
                    [
                        jnp.broadcast_to(scale_rows[block, 2 * j + i : 2 * j + i + 1, :], (ROWS // 2, HEAD_DIM))
                        for i in range(2)
                    ],
                    axis=0,
                )
                result = result + part * factor
            numer[j] = result

        all_keys = [make_keys(j) for j in range(PAIRS)]
        all_scores = [make_scores(j, all_keys[j]) for j in range(PAIRS)]
        weighed = [weigh(j, all_scores[j]) for j in range(PAIRS)]
        for j in range(PAIRS):
            add_values(j, *weighed[j])

    for j in range(PAIRS):
        total[j] = jnp.broadcast_to(jnp.sum(total[j], axis=1, keepdims=True), (ROWS, HEAD_DIM))
    half = PAIRS // 2
    for ref, first in ((mine_ref, kv_at * half), (send_ref, (1 - kv_at) * half)):
        for part, state in enumerate((numer, peak, total)):
            for i in range(half):
                whole = state[first + i]
                for h in range(ROWS // Q_TOK):
                    column = (i * (ROWS // Q_TOK) + h) * HEAD_DIM
                    ref[part, :, column : column + HEAD_DIM] = whole[h * Q_TOK : (h + 1) * Q_TOK]


def attend(length, latents, codes, scales, queries, new_keys, new_values, key_factor):
    f32, bf16 = jnp.float32, jnp.bfloat16
    vmem = pl.BlockSpec(memory_space=pltpu.VMEM)
    hbm = pl.BlockSpec(memory_space=pltpu.HBM)
    shape = jax.ShapeDtypeStruct((3, Q_TOK, HEADS // 2 * HEAD_DIM), f32)
    macs = CTX_DEV * (RANK * KV_HEADS + 2 * PAIRS * ROWS * 2) * HEAD_DIM
    width = KV_HEADS * HEAD_DIM
    return pl.pallas_call(
        attend_kernel,
        out_shape=(shape, shape),
        in_specs=[pl.BlockSpec(memory_space=pltpu.SMEM)] + [hbm] * 8,
        out_specs=(vmem, vmem),
        scratch_shapes=[
            pltpu.VMEM((RANK, CTX_DEV), bf16),
            pltpu.VMEM((CTX_DEV, width), bf16),
            pltpu.VMEM((2, HALF, CTX_DEV), f32),
            pltpu.VMEM((KV_HEADS, CTX_DEV // BLK), bf16),
            pltpu.VMEM((Q_TOK, HEADS * HEAD_DIM), bf16),
            pltpu.VMEM((Q_TOK, width), bf16),
            pltpu.VMEM((Q_TOK, width), bf16),
            pltpu.VMEM((RANK, width), bf16),
            pltpu.SemaphoreType.DMA((N_CHUNKS,)),
            pltpu.SemaphoreType.DMA((N_CHUNKS,)),
            pltpu.SemaphoreType.DMA((N_CHUNKS,)),
            pltpu.SemaphoreType.DMA((5,)),
            pltpu.VMEM((PAIRS, ROWS, 2 * HEAD_DIM), bf16),
            pltpu.VMEM((width, RANK), bf16),
            pltpu.VMEM((CTX_DEV // BLK, KV_HEADS, HEAD_DIM), f32),
            pltpu.VMEM((PAIRS, ROWS, HEAD_DIM), f32),
            pltpu.VMEM((PAIRS, ROWS, HEAD_DIM), f32),
            pltpu.VMEM((PAIRS, ROWS, HEAD_DIM), f32),
        ],
        compiler_params=pltpu.CompilerParams(vmem_limit_bytes=36 * 2**20),
        cost_estimate=pl.CostEstimate(
            flops=2 * macs, bytes_accessed=12 * 2**20, transcendentals=CTX_DEV * HEADS * Q_TOK
        ),
        name="attend",
    )(length, *[
        pltpu.with_memory_space_constraint(x, pltpu.HBM)
        for x in (latents.T, codes, jnp.asarray(rotary_table()), scales.T, queries, new_keys, new_values, key_factor)
    ])


def merge(a, b):
    top = jnp.maximum(a[1], b[1])
    weight_a, weight_b = (jnp.exp2((x[1] - top) * EXP2_SCALE) for x in (a, b))
    numer = a[0] * weight_a + b[0] * weight_b
    return (numer / (a[2] * weight_a + b[2] * weight_b)).astype(jnp.bfloat16)


def other_core(x):
    return lax.ppermute(x, "kv", [(0, 1), (1, 0)])


AXES = {"z": 16, "y": 4, "x": 1}
SIDE = 4
WEIGHT_AXIS = ("x", "y")
FIRST_AXIS = ("y", "z")
SECOND_AXIS = ("z", "x")
SHIFTS = (1, -1, 2)


def coordinate(chip, axis):
    return chip // AXES[axis] % SIDE


def shifted(x, axes, shift):
    moves = []
    for chip in range(SIDE**3):
        for core, axis in enumerate(axes):
            at = coordinate(chip, axis)
            target = chip + ((at + shift) % SIDE - at) * AXES[axis]
            moves.append((chip * 2 + core, target * 2 + core))
    return lax.ppermute(x, ("group", "kv"), moves)


def gathered(x, axes):
    return jnp.concatenate([x] + [shifted(x, axes, shift) for shift in SHIFTS], axis=0)


def assemble_kernel(*refs):
    *pieces, out_ref, whole = refs
    chip, core = lax.axis_index("group"), lax.axis_index("kv")
    steps = (0,) + SHIFTS

    def place(axes, at_core, shift):
        value = jnp.int32(0)
        for c, axis in enumerate(axes):
            at = lax.rem(lax.div(chip, AXES[axis]) + (shift + SIDE), SIDE) * AXES[axis]
            value = jnp.where(at_core == c, at, value)
        return value

    for at_core, refs in ((core, pieces[: len(steps)]), (1 - core, pieces[len(steps) :])):
        for ref, d in zip(refs, steps):
            for i, e in enumerate(steps):
                for j, f in enumerate(steps):
                    request = (
                        place(WEIGHT_AXIS, at_core, d)
                        + place(FIRST_AXIS, at_core, -f)
                        + place(SECOND_AXIS, at_core, -e)
                    )
                    row = (i * SIDE + j) * Q_TOK
                    at = pl.ds(pl.multiple_of(request * Q_TOK, Q_TOK), Q_TOK)
                    block = ref[row : row + Q_TOK, :]
                    whole[at, :] = block if at_core is core else whole[at, :] + block
    half = out_ref.shape[0]
    out_ref[...] = whole[pl.ds(pl.multiple_of(core * half, half), half), :]


def assemble(own, other):
    vmem = pl.BlockSpec(memory_space=pltpu.VMEM)
    rows, columns = SIDE * own[0].shape[0], own[0].shape[1]
    return pl.pallas_call(
        assemble_kernel,
        out_shape=jax.ShapeDtypeStruct((rows // 2, columns), jnp.float32),
        in_specs=[vmem] * 8,
        out_specs=vmem,
        scratch_shapes=[pltpu.VMEM((rows, columns), jnp.float32)],
        compiler_params=pltpu.CompilerParams(vmem_limit_bytes=4 * 2**20),
        name="assemble",
    )(*own, *other)


def body(lengths, latents, codes, scales, queries, new_keys, new_values, key_factor, out_weight):
    half = out_weight.shape[0] // 2
    before, after = (shifted(out_weight, WEIGHT_AXIS, shift) for shift in SHIFTS[:2])
    mine, send = attend(
        lengths, latents[0], codes[0], scales[0], queries[0], new_keys[0], new_values[0], key_factor
    )
    mine, before, after = lax.optimization_barrier((mine, before, after))
    far = [shifted(before[:half], WEIGHT_AXIS, 1), shifted(after[half:], WEIGHT_AXIS, -1)]
    attended = merge(mine, other_core(send))
    rows = gathered(gathered(attended[None], FIRST_AXIS), SECOND_AXIS)
    rows = rows.reshape(SIDE * SIDE * Q_TOK, HEADS // 2 * HEAD_DIM)
    results = [dot(rows, w) for w in (out_weight, before, after)]
    results.append(dot(rows[:, :half], far[0]) + dot(rows[:, half:], far[1]))
    pieces = [results[0]] + [shifted(r, WEIGHT_AXIS, -shift) for r, shift in zip(results[1:], SHIFTS)]
    return assemble(pieces, [other_core(p) for p in pieces])


def solution(mesh):
    placed = (
        P("group"),
        P("group", "kv", None),
        P("group", "kv", None),
        P("group", "kv", None),
        P("group", None, None),
        P("group", None, None),
        P("group", None, None),
        P(),
        P("kv", "group"),
    )
    return jax.shard_map(
        body, mesh=mesh, in_specs=placed, out_specs=P("kv", "group"), check_vma=False
    )
```

```python
import functools

import jax
import jax.numpy as jnp
import numpy as np
from jax import lax
from jax.experimental import pallas as pl
from jax.experimental.pallas import tpu as pltpu
from jax.sharding import PartitionSpec as P

HEADS = 64
KV_HEADS = 8
HEAD_DIM = 128
HALF = HEAD_DIM // 2
RANK = 160
BLK = 256
CTX_DEV = 4096
Q_TOK = 8
PAIRS = KV_HEADS // 2
ROWS = 2 * (HEADS // KV_HEADS) * Q_TOK
CHUNK = 2048
N_CHUNKS = CTX_DEV // CHUNK
ROPE_BASE = 500000.0
NEG_FILL = -1e30
EXP2_SCALE = float(HEAD_DIM**-0.5 * np.log2(np.e))


def rotary_table():
    freq = np.float32(ROPE_BASE) ** (-(np.arange(HALF, dtype=np.float32) * 2.0) / HEAD_DIM)
    angles = np.arange(2 * CTX_DEV, dtype=np.float32)[None, :] * freq.astype(np.float32)[:, None]
    angles = angles.reshape(HALF, 2, CTX_DEV).astype(np.float64)
    return np.stack([np.cos(angles), np.sin(angles)]).transpose(2, 0, 1, 3).astype(np.float32)


STRIP = 16


def strip_order():
    starts = [
        head * HEAD_DIM + half * HALF + m * STRIP
        for m in range(HALF // STRIP)
        for head in range(2)
        for half in range(2)
    ]
    return np.concatenate([np.arange(a, a + STRIP) for a in starts])


def dot(a, b):
    return jnp.dot(a, b, preferred_element_type=jnp.float32)


def own_blocks(x):
    return jnp.concatenate([x[: ROWS // 2, :HEAD_DIM], x[ROWS // 2 :, HEAD_DIM:]], axis=0)


def attend_kernel(
    length_ref, lat_hbm, code_hbm, table_hbm, scale_hbm, q_hbm, nk_hbm, nv_hbm, kf_hbm,
    mine_ref, send_ref,
    lat_buf, code_buf, table_buf, scale_buf, q_buf, nk_buf, nv_buf, kf_buf,
    lat_sem, code_sem, table_sem, small_sem,
    qc, wt, scale_rows, peak, total, numer, scores,
):
    f32, bf16 = jnp.float32, jnp.bfloat16
    kv_at = lax.axis_index("kv")
    valid = jnp.clip(length_ref[0] - kv_at * CTX_DEV, 0, CTX_DEV)
    chunks = lax.div(valid + (CHUNK - 1), CHUNK)

    small = [
        pltpu.make_async_copy(src, dst, small_sem.at[i])
        for i, (src, dst) in enumerate(
            ((kf_hbm, kf_buf), (q_hbm, q_buf), (nk_hbm, nk_buf), (nv_hbm, nv_buf), (scale_hbm, scale_buf))
        )
    ]
    for copy in small:
        copy.start()

    def at(c):
        return pl.ds(pl.multiple_of(c * CHUNK, CHUNK), CHUNK)

    def key_copies(c):
        return (
            pltpu.make_async_copy(lat_hbm.at[:, at(c)], lat_buf.at[:, at(c)], lat_sem.at[c]),
            pltpu.make_async_copy(table_hbm.at[kv_at, :, :, at(c)], table_buf.at[:, :, at(c)], table_sem.at[c]),
        )

    def code_copy(c):
        return pltpu.make_async_copy(code_hbm.at[at(c)], code_buf.at[at(c)], code_sem.at[c])

    @pl.loop(0, chunks)
    def _(c):
        for copy in key_copies(c):
            copy.start()

    @pl.loop(0, chunks)
    def _(c):
        code_copy(c).start()

    for copy in small:
        copy.wait()
    scales = scale_buf[...].astype(f32)
    for b in range(CTX_DEV // BLK):
        scale_rows[b] = jnp.broadcast_to(scales[:, b : b + 1], (KV_HEADS, HEAD_DIM))
    row_tok = lax.rem(lax.broadcasted_iota(jnp.int32, (ROWS, HEAD_DIM), 0), Q_TOK)
    lane = lax.broadcasted_iota(jnp.int32, (ROWS, HEAD_DIM), 1)
    causal = jnp.logical_and(lane <= row_tok, kv_at == 0)
    queries = q_buf[...].astype(f32)
    new_keys = nk_buf[...].astype(f32)
    new_values = nv_buf[...].astype(f32)
    pad = jnp.zeros((HEAD_DIM - Q_TOK, 2 * HEAD_DIM), f32)
    groups = HEADS // KV_HEADS
    blank = jnp.zeros((ROWS // 2, HEAD_DIM), f32)

    def head_rows(k):
        return jnp.concatenate(
            [queries[:, (k * groups + g) * HEAD_DIM : (k * groups + g + 1) * HEAD_DIM] for g in range(groups)],
            axis=0,
        )

    order = strip_order()
    source = lax.broadcasted_iota(jnp.int32, (2 * HEAD_DIM, 2 * HEAD_DIM), 0)
    target = lax.broadcasted_iota(jnp.int32, (2 * HEAD_DIM, 2 * HEAD_DIM), 1)
    strip, inside = lax.div(target, STRIP), lax.rem(target, STRIP)
    wanted = (
        lax.rem(lax.div(strip, 2), 2) * HEAD_DIM + lax.rem(strip, 2) * HALF + lax.div(strip, 4) * STRIP + inside
    )
    arrange = jnp.where(source == wanted, 1.0, 0.0).astype(bf16)

    for j in range(PAIRS):
        columns = slice(2 * j * HEAD_DIM, (2 * j + 2) * HEAD_DIM)
        plain = jnp.concatenate(
            [
                jnp.concatenate([head_rows(2 * j), blank], axis=1),
                jnp.concatenate([blank, head_rows(2 * j + 1)], axis=1),
            ],
            axis=0,
        ).astype(bf16)
        qc[j] = dot(plain, arrange).astype(bf16)
        turned = kf_buf[:, columns].astype(f32).T
        wt[columns, :] = jnp.concatenate(
            [turned[a : a + STRIP] for a in order[::STRIP]], axis=0
        ).astype(bf16)
        fresh_keys = jnp.concatenate([new_keys[:, columns], pad], axis=0).astype(bf16)
        fresh_values = jnp.concatenate([new_values[:, columns], pad], axis=0).astype(bf16)
        s = lax.dot_general(plain, fresh_keys, (((1,), (1,)), ((), ())), preferred_element_type=f32)
        s = jnp.where(causal, s, NEG_FILL)
        top = jnp.broadcast_to(jnp.max(s, axis=1, keepdims=True), s.shape)
        weights = jnp.where(causal, jnp.exp2((s - top) * EXP2_SCALE), 0.0)
        peak[j] = top
        total[j] = weights
        numer[j] = own_blocks(dot(weights.astype(bf16), fresh_values))

    def make_keys(c):
        for copy in key_copies(c):
            copy.wait()
        lat = lat_buf[:, at(c)]
        every = []
        for j in range(PAIRS):
            columns = slice(2 * j * HEAD_DIM, (2 * j + 2) * HEAD_DIM)
            cos, sin = table_buf[0, :, at(c)], table_buf[1, :, at(c)]
            pre = dot(wt[columns, :], lat)
            keys = []
            for m in range(HALF // STRIP):
                here = slice(m * STRIP, (m + 1) * STRIP)
                for i in range(2):
                    at_lo = (4 * m + 2 * i) * STRIP
                    lo, hi = pre[at_lo : at_lo + STRIP], pre[at_lo + STRIP : at_lo + 2 * STRIP]
                    keys.append((lo * cos[here] - hi * sin[here]).astype(bf16))
                    keys.append((hi * cos[here] + lo * sin[here]).astype(bf16))
            every.append(jnp.concatenate(keys, axis=0))
        return every

    def make_scores(c, keys):
        position = c * CHUNK + lax.broadcasted_iota(jnp.int32, (1, CHUNK), 1)
        hide = jnp.where(position < valid, 0.0, NEG_FILL)
        for j in range(PAIRS):
            scores[j] = dot(qc[j], keys[j]) + hide

    def weigh(j):
        s = scores[j]
        old = peak[j]
        new = jnp.maximum(old, jnp.max(s, axis=1, keepdims=True))
        shrink = jnp.exp2((old - new) * EXP2_SCALE)
        weights = [
            jnp.exp2((s[:, i : i + HEAD_DIM] - new) * EXP2_SCALE) for i in range(0, CHUNK, HEAD_DIM)
        ]
        peak[j] = new
        total[j] = total[j] * shrink + functools.reduce(jnp.add, weights)
        return shrink, [w.astype(bf16) for w in weights]

    def add_values(c, j, shrink, rounded):
        columns = slice(2 * j * HEAD_DIM, (2 * j + 2) * HEAD_DIM)
        result = numer[j] * shrink
        for b in range(CHUNK // BLK):
            per = BLK // HEAD_DIM
            w = jnp.concatenate(rounded[b * per : (b + 1) * per], axis=1)
            v = code_buf[pl.ds(pl.multiple_of(c * CHUNK + b * BLK, BLK), BLK), columns]
            part = own_blocks(dot(w, v))
            block = c * (CHUNK // BLK) + b
            factor = jnp.concatenate(
                [
                    jnp.broadcast_to(scale_rows[block, 2 * j + i : 2 * j + i + 1, :], (ROWS // 2, HEAD_DIM))
                    for i in range(2)
                ],
                axis=0,
            )
            result = result + part * factor
        numer[j] = result

    @pl.when(chunks > 0)
    def _():
        make_scores(0, make_keys(0))

    @pl.loop(0, chunks - 1)
    def _(c):
        code_copy(c).wait()
        keys = make_keys(c + 1)
        weighed = [weigh(j) for j in range(PAIRS)]
        make_scores(c + 1, keys)
        for j in range(PAIRS):
            add_values(c, j, *weighed[j])

    @pl.when(chunks > 0)
    def _():
        code_copy(chunks - 1).wait()
        weighed = [weigh(j) for j in range(PAIRS)]
        for j in range(PAIRS):
            add_values(chunks - 1, j, *weighed[j])

    for j in range(PAIRS):
        total[j] = jnp.broadcast_to(jnp.sum(total[j], axis=1, keepdims=True), (ROWS, HEAD_DIM))
    half = PAIRS // 2
    for ref, first in ((mine_ref, kv_at * half), (send_ref, (1 - kv_at) * half)):
        for part, state in enumerate((numer, peak, total)):
            for i in range(half):
                whole = state[first + i]
                for h in range(ROWS // Q_TOK):
                    column = (i * (ROWS // Q_TOK) + h) * HEAD_DIM
                    ref[part, :, column : column + HEAD_DIM] = whole[h * Q_TOK : (h + 1) * Q_TOK]


def attend(length, latents, codes, scales, queries, new_keys, new_values, key_factor):
    f32, bf16 = jnp.float32, jnp.bfloat16
    vmem = pl.BlockSpec(memory_space=pltpu.VMEM)
    hbm = pl.BlockSpec(memory_space=pltpu.HBM)
    shape = jax.ShapeDtypeStruct((3, Q_TOK, HEADS // 2 * HEAD_DIM), f32)
    macs = CTX_DEV * (RANK * KV_HEADS + 2 * PAIRS * ROWS * 2) * HEAD_DIM
    width = KV_HEADS * HEAD_DIM
    return pl.pallas_call(
        attend_kernel,
        out_shape=(shape, shape),
        in_specs=[pl.BlockSpec(memory_space=pltpu.SMEM)] + [hbm] * 8,
        out_specs=(vmem, vmem),
        scratch_shapes=[
            pltpu.VMEM((RANK, CTX_DEV), bf16),
            pltpu.VMEM((CTX_DEV, width), bf16),
            pltpu.VMEM((2, HALF, CTX_DEV), f32),
            pltpu.VMEM((KV_HEADS, CTX_DEV // BLK), bf16),
            pltpu.VMEM((Q_TOK, HEADS * HEAD_DIM), bf16),
            pltpu.VMEM((Q_TOK, width), bf16),
            pltpu.VMEM((Q_TOK, width), bf16),
            pltpu.VMEM((RANK, width), bf16),
            pltpu.SemaphoreType.DMA((N_CHUNKS,)),
            pltpu.SemaphoreType.DMA((N_CHUNKS,)),
            pltpu.SemaphoreType.DMA((N_CHUNKS,)),
            pltpu.SemaphoreType.DMA((5,)),
            pltpu.VMEM((PAIRS, ROWS, 2 * HEAD_DIM), bf16),
            pltpu.VMEM((width, RANK), bf16),
            pltpu.VMEM((CTX_DEV // BLK, KV_HEADS, HEAD_DIM), f32),
            pltpu.VMEM((PAIRS, ROWS, HEAD_DIM), f32),
            pltpu.VMEM((PAIRS, ROWS, HEAD_DIM), f32),
            pltpu.VMEM((PAIRS, ROWS, HEAD_DIM), f32),
            pltpu.VMEM((PAIRS, ROWS, CHUNK), f32),
        ],
        compiler_params=pltpu.CompilerParams(vmem_limit_bytes=36 * 2**20),
        cost_estimate=pl.CostEstimate(
            flops=2 * macs, bytes_accessed=12 * 2**20, transcendentals=CTX_DEV * HEADS * Q_TOK
        ),
        name="attend",
    )(length, *[
        pltpu.with_memory_space_constraint(x, pltpu.HBM)
        for x in (latents.T, codes, jnp.asarray(rotary_table()), scales.T, queries, new_keys, new_values, key_factor)
    ])


def merge(a, b):
    top = jnp.maximum(a[1], b[1])
    weight_a, weight_b = (jnp.exp2((x[1] - top) * EXP2_SCALE) for x in (a, b))
    numer = a[0] * weight_a + b[0] * weight_b
    return (numer / (a[2] * weight_a + b[2] * weight_b)).astype(jnp.bfloat16)


def other_core(x):
    return lax.ppermute(x, "kv", [(0, 1), (1, 0)])


AXES = {"z": 16, "y": 4, "x": 1}
SIDE = 4
WEIGHT_AXIS = ("x", "y")
FIRST_AXIS = ("y", "z")
SECOND_AXIS = ("z", "x")
SHIFTS = (1, -1, 2)
FIRST_SHIFTS = (2, 1, -1)


def coordinate(chip, axis):
    return chip // AXES[axis] % SIDE


def shifted(x, axes, shift):
    moves = []
    for chip in range(SIDE**3):
        for core, axis in enumerate(axes):
            at = coordinate(chip, axis)
            target = chip + ((at + shift) % SIDE - at) * AXES[axis]
            moves.append((chip * 2 + core, target * 2 + core))
    return lax.ppermute(x, ("group", "kv"), moves)


def gathered(x, axes):
    return jnp.concatenate([x] + [shifted(x, axes, shift) for shift in SHIFTS], axis=0)


def assemble_kernel(*refs):
    *pieces, out_ref, whole = refs
    chip, core = lax.axis_index("group"), lax.axis_index("kv")
    steps = (0,) + SHIFTS

    def place(axes, at_core, shift):
        value = jnp.int32(0)
        for c, axis in enumerate(axes):
            at = lax.rem(lax.div(chip, AXES[axis]) + (shift + SIDE), SIDE) * AXES[axis]
            value = jnp.where(at_core == c, at, value)
        return value

    for at_core, refs in ((core, pieces[: len(steps)]), (1 - core, pieces[len(steps) :])):
        for ref, d in zip(refs, steps):
            for i, e in enumerate(steps):
                for j, f in enumerate((0,) + FIRST_SHIFTS):
                    request = (
                        place(WEIGHT_AXIS, at_core, d)
                        + place(FIRST_AXIS, at_core, -f)
                        + place(SECOND_AXIS, at_core, -e)
                    )
                    row = (i * SIDE + j) * Q_TOK
                    at = pl.ds(pl.multiple_of(request * Q_TOK, Q_TOK), Q_TOK)
                    block = ref[row : row + Q_TOK, :]
                    whole[at, :] = block if at_core is core else whole[at, :] + block
    half = out_ref.shape[0]
    out_ref[...] = whole[pl.ds(pl.multiple_of(core * half, half), half), :]


def assemble(own, other):
    vmem = pl.BlockSpec(memory_space=pltpu.VMEM)
    rows, columns = SIDE * own[0].shape[0], own[0].shape[1]
    return pl.pallas_call(
        assemble_kernel,
        out_shape=jax.ShapeDtypeStruct((rows // 2, columns), jnp.float32),
        in_specs=[vmem] * 8,
        out_specs=vmem,
        scratch_shapes=[pltpu.VMEM((rows, columns), jnp.float32)],
        compiler_params=pltpu.CompilerParams(vmem_limit_bytes=4 * 2**20),
        name="assemble",
    )(*own, *other)


def body(lengths, latents, codes, scales, queries, new_keys, new_values, key_factor, out_weight):
    cut = out_weight.shape[0] // 16
    before, after = (shifted(out_weight, WEIGHT_AXIS, shift) for shift in SHIFTS[:2])
    mine, send = attend(
        lengths, latents[0], codes[0], scales[0], queries[0], new_keys[0], new_values[0], key_factor
    )
    attended = merge(mine, [other_core(part) for part in send])
    before, after = lax.optimization_barrier((before, after))
    half = out_weight.shape[0] // 2
    far = [
        shifted(before[:cut], WEIGHT_AXIS, 1),
        shifted(before[cut:half], WEIGHT_AXIS, 1),
        shifted(after[half:], WEIGHT_AXIS, -1),
    ]
    blocks = [attended[None]] + [shifted(attended[None], FIRST_AXIS, shift) for shift in FIRST_SHIFTS]
    blocks[1], far[0] = lax.optimization_barrier((blocks[1], far[0]))
    rows = gathered(jnp.concatenate(blocks, axis=0), SECOND_AXIS)
    rows = rows.reshape(SIDE * SIDE * Q_TOK, HEADS // 2 * HEAD_DIM)
    results = [dot(rows, w) for w in (out_weight, before, after)]
    results.append(dot(rows[:, :cut], far[0]) + dot(rows[:, cut:half], far[1]) + dot(rows[:, half:], far[2]))
    pieces = [results[0]] + [shifted(r, WEIGHT_AXIS, -shift) for r, shift in zip(results[1:], SHIFTS)]
    return assemble(pieces, [other_core(p) for p in pieces])


def solution(mesh):
    placed = (
        P("group"),
        P("group", "kv", None),
        P("group", "kv", None),
        P("group", "kv", None),
        P("group", None, None),
        P("group", None, None),
        P("group", None, None),
        P(),
        P("kv", "group"),
    )
    return jax.shard_map(
        body, mesh=mesh, in_specs=placed, out_specs=P("kv", "group"), check_vma=False
    )
```

```python
import functools

import jax
import jax.numpy as jnp
import numpy as np
from jax import lax
from jax.experimental import pallas as pl
from jax.experimental.pallas import tpu as pltpu
from jax.sharding import PartitionSpec as P

HEADS = 64
KV_HEADS = 8
HEAD_DIM = 128
HALF = HEAD_DIM // 2
RANK = 160
BLK = 256
CTX_DEV = 4096
Q_TOK = 8
PAIRS = KV_HEADS // 2
ROWS = 2 * (HEADS // KV_HEADS) * Q_TOK
CHUNK = 2048
N_CHUNKS = CTX_DEV // CHUNK
ROPE_BASE = 500000.0
NEG_FILL = -1e30
EXP2_SCALE = float(HEAD_DIM**-0.5 * np.log2(np.e))


def rotary_table():
    freq = np.float32(ROPE_BASE) ** (-(np.arange(HALF, dtype=np.float32) * 2.0) / HEAD_DIM)
    angles = np.arange(2 * CTX_DEV, dtype=np.float32)[None, :] * freq.astype(np.float32)[:, None]
    angles = angles.reshape(HALF, 2, CTX_DEV).astype(np.float64)
    return np.stack([np.cos(angles), np.sin(angles)]).transpose(2, 0, 1, 3).astype(np.float32)


STRIP = 16


def strip_order():
    starts = [
        head * HEAD_DIM + half * HALF + m * STRIP
        for m in range(HALF // STRIP)
        for head in range(2)
        for half in range(2)
    ]
    return np.concatenate([np.arange(a, a + STRIP) for a in starts])


def dot(a, b):
    return jnp.dot(a, b, preferred_element_type=jnp.float32)


def own_blocks(x):
    return jnp.concatenate([x[: ROWS // 2, :HEAD_DIM], x[ROWS // 2 :, HEAD_DIM:]], axis=0)


def attend_kernel(
    length_ref, lat_hbm, code_hbm, table_hbm, scale_hbm, q_hbm, nk_hbm, nv_hbm, kf_hbm,
    mine_ref, send_ref,
    lat_buf, code_buf, table_buf, scale_buf, q_buf, nk_buf, nv_buf, kf_buf,
    lat_sem, code_sem, table_sem, small_sem,
    qc, wt, scale_rows, peak, total, numer, scores,
):
    f32, bf16 = jnp.float32, jnp.bfloat16
    kv_at = lax.axis_index("kv")
    valid = jnp.clip(length_ref[0] - kv_at * CTX_DEV, 0, CTX_DEV)
    chunks = lax.div(valid + (CHUNK - 1), CHUNK)

    small = [
        pltpu.make_async_copy(src, dst, small_sem.at[i])
        for i, (src, dst) in enumerate(
            ((kf_hbm, kf_buf), (q_hbm, q_buf), (nk_hbm, nk_buf), (nv_hbm, nv_buf), (scale_hbm, scale_buf))
        )
    ]
    for copy in small:
        copy.start()

    def at(c):
        return pl.ds(pl.multiple_of(c * CHUNK, CHUNK), CHUNK)

    def key_copies(c):
        return (
            pltpu.make_async_copy(lat_hbm.at[:, at(c)], lat_buf.at[:, at(c)], lat_sem.at[c]),
            pltpu.make_async_copy(table_hbm.at[kv_at, :, :, at(c)], table_buf.at[:, :, at(c)], table_sem.at[c]),
        )

    def code_copy(c):
        return pltpu.make_async_copy(code_hbm.at[at(c)], code_buf.at[at(c)], code_sem.at[c])

    @pl.loop(0, chunks)
    def _(c):
        for copy in key_copies(c):
            copy.start()

    @pl.loop(0, chunks)
    def _(c):
        code_copy(c).start()

    for copy in small:
        copy.wait()
    scales = scale_buf[...].astype(f32)
    for b in range(CTX_DEV // BLK):
        scale_rows[b] = jnp.broadcast_to(scales[:, b : b + 1], (KV_HEADS, HEAD_DIM))
    row_tok = lax.rem(lax.broadcasted_iota(jnp.int32, (ROWS, HEAD_DIM), 0), Q_TOK)
    lane = lax.broadcasted_iota(jnp.int32, (ROWS, HEAD_DIM), 1)
    causal = jnp.logical_and(lane <= row_tok, kv_at == 0)
    queries = q_buf[...].astype(f32)
    new_keys = nk_buf[...].astype(f32)
    new_values = nv_buf[...].astype(f32)
    pad = jnp.zeros((HEAD_DIM - Q_TOK, 2 * HEAD_DIM), f32)
    groups = HEADS // KV_HEADS
    blank = jnp.zeros((ROWS // 2, HEAD_DIM), f32)

    def head_rows(k):
        return jnp.concatenate(
            [queries[:, (k * groups + g) * HEAD_DIM : (k * groups + g + 1) * HEAD_DIM] for g in range(groups)],
            axis=0,
        )

    order = strip_order()
    source = lax.broadcasted_iota(jnp.int32, (2 * HEAD_DIM, 2 * HEAD_DIM), 0)
    target = lax.broadcasted_iota(jnp.int32, (2 * HEAD_DIM, 2 * HEAD_DIM), 1)
    strip, inside = lax.div(target, STRIP), lax.rem(target, STRIP)
    wanted = (
        lax.rem(lax.div(strip, 2), 2) * HEAD_DIM + lax.rem(strip, 2) * HALF + lax.div(strip, 4) * STRIP + inside
    )
    arrange = jnp.where(source == wanted, 1.0, 0.0).astype(bf16)

    for j in range(PAIRS):
        columns = slice(2 * j * HEAD_DIM, (2 * j + 2) * HEAD_DIM)
        plain = jnp.concatenate(
            [
                jnp.concatenate([head_rows(2 * j), blank], axis=1),
                jnp.concatenate([blank, head_rows(2 * j + 1)], axis=1),
            ],
            axis=0,
        ).astype(bf16)
        qc[j] = dot(plain, arrange).astype(bf16)
        turned = kf_buf[:, columns].astype(f32).T
        wt[columns, :] = jnp.concatenate(
            [turned[a : a + STRIP] for a in order[::STRIP]], axis=0
        ).astype(bf16)
        fresh_keys = jnp.concatenate([new_keys[:, columns], pad], axis=0).astype(bf16)
        fresh_values = jnp.concatenate([new_values[:, columns], pad], axis=0).astype(bf16)
        s = lax.dot_general(plain, fresh_keys, (((1,), (1,)), ((), ())), preferred_element_type=f32)
        s = jnp.where(causal, s, NEG_FILL)
        top = jnp.broadcast_to(jnp.max(s, axis=1, keepdims=True), s.shape)
        weights = jnp.where(causal, jnp.exp2((s - top) * EXP2_SCALE), 0.0)
        peak[j] = top
        total[j] = weights
        numer[j] = own_blocks(dot(weights.astype(bf16), fresh_values))

    def make_keys(c):
        for copy in key_copies(c):
            copy.wait()
        lat = lat_buf[:, at(c)]
        every = []
        for j in range(PAIRS):
            columns = slice(2 * j * HEAD_DIM, (2 * j + 2) * HEAD_DIM)
            cos, sin = table_buf[0, :, at(c)], table_buf[1, :, at(c)]
            pre = dot(wt[columns, :], lat)
            keys = []
            for m in range(HALF // STRIP):
                here = slice(m * STRIP, (m + 1) * STRIP)
                for i in range(2):
                    at_lo = (4 * m + 2 * i) * STRIP
                    lo, hi = pre[at_lo : at_lo + STRIP], pre[at_lo + STRIP : at_lo + 2 * STRIP]
                    keys.append((lo * cos[here] - hi * sin[here]).astype(bf16))
                    keys.append((hi * cos[here] + lo * sin[here]).astype(bf16))
            every.append(jnp.concatenate(keys, axis=0))
        return every

    def make_scores(c, keys):
        position = c * CHUNK + lax.broadcasted_iota(jnp.int32, (1, CHUNK), 1)
        hide = jnp.where(position < valid, 0.0, NEG_FILL)
        for j in range(PAIRS):
            scores[j] = dot(qc[j], keys[j]) + hide

    def weigh(j):
        s = scores[j]
        old = peak[j]
        new = jnp.maximum(old, jnp.max(s, axis=1, keepdims=True))
        shrink = jnp.exp2((old - new) * EXP2_SCALE)
        weights = [
            jnp.exp2((s[:, i : i + HEAD_DIM] - new) * EXP2_SCALE) for i in range(0, CHUNK, HEAD_DIM)
        ]
        peak[j] = new
        total[j] = total[j] * shrink + functools.reduce(jnp.add, weights)
        return shrink, [w.astype(bf16) for w in weights]

    def add_values(c, j, shrink, rounded):
        columns = slice(2 * j * HEAD_DIM, (2 * j + 2) * HEAD_DIM)
        result = numer[j] * shrink
        for b in range(CHUNK // BLK):
            per = BLK // HEAD_DIM
            w = jnp.concatenate(rounded[b * per : (b + 1) * per], axis=1)
            v = code_buf[pl.ds(pl.multiple_of(c * CHUNK + b * BLK, BLK), BLK), columns]
            part = own_blocks(dot(w, v))
            block = c * (CHUNK // BLK) + b
            factor = jnp.concatenate(
                [
                    jnp.broadcast_to(scale_rows[block, 2 * j + i : 2 * j + i + 1, :], (ROWS // 2, HEAD_DIM))
                    for i in range(2)
                ],
                axis=0,
            )
            result = result + part * factor
        numer[j] = result

    @pl.when(chunks > 0)
    def _():
        make_scores(0, make_keys(0))

    @pl.loop(0, chunks - 1)
    def _(c):
        code_copy(c).wait()
        keys = make_keys(c + 1)
        weighed = [weigh(j) for j in range(PAIRS)]
        make_scores(c + 1, keys)
        for j in range(PAIRS):
            add_values(c, j, *weighed[j])

    @pl.when(chunks > 0)
    def _():
        code_copy(chunks - 1).wait()
        weighed = [weigh(j) for j in range(PAIRS)]
        for j in range(PAIRS):
            add_values(chunks - 1, j, *weighed[j])

    for j in range(PAIRS):
        total[j] = jnp.broadcast_to(jnp.sum(total[j], axis=1, keepdims=True), (ROWS, HEAD_DIM))
    half = PAIRS // 2
    for ref, first in ((mine_ref, kv_at * half), (send_ref, (1 - kv_at) * half)):
        for part, state in enumerate((numer, peak, total)):
            for i in range(half):
                whole = state[first + i]
                for h in range(ROWS // Q_TOK):
                    column = (i * (ROWS // Q_TOK) + h) * HEAD_DIM
                    ref[part, :, column : column + HEAD_DIM] = whole[h * Q_TOK : (h + 1) * Q_TOK]


def attend(length, latents, codes, scales, queries, new_keys, new_values, key_factor):
    f32, bf16 = jnp.float32, jnp.bfloat16
    vmem = pl.BlockSpec(memory_space=pltpu.VMEM)
    hbm = pl.BlockSpec(memory_space=pltpu.HBM)
    shape = jax.ShapeDtypeStruct((3, Q_TOK, HEADS // 2 * HEAD_DIM), f32)
    macs = CTX_DEV * (RANK * KV_HEADS + 2 * PAIRS * ROWS * 2) * HEAD_DIM
    width = KV_HEADS * HEAD_DIM
    return pl.pallas_call(
        attend_kernel,
        out_shape=(shape, shape),
        in_specs=[pl.BlockSpec(memory_space=pltpu.SMEM)] + [hbm] * 8,
        out_specs=(vmem, vmem),
        scratch_shapes=[
            pltpu.VMEM((RANK, CTX_DEV), bf16),
            pltpu.VMEM((CTX_DEV, width), bf16),
            pltpu.VMEM((2, HALF, CTX_DEV), f32),
            pltpu.VMEM((KV_HEADS, CTX_DEV // BLK), bf16),
            pltpu.VMEM((Q_TOK, HEADS * HEAD_DIM), bf16),
            pltpu.VMEM((Q_TOK, width), bf16),
            pltpu.VMEM((Q_TOK, width), bf16),
            pltpu.VMEM((RANK, width), bf16),
            pltpu.SemaphoreType.DMA((N_CHUNKS,)),
            pltpu.SemaphoreType.DMA((N_CHUNKS,)),
            pltpu.SemaphoreType.DMA((N_CHUNKS,)),
            pltpu.SemaphoreType.DMA((5,)),
            pltpu.VMEM((PAIRS, ROWS, 2 * HEAD_DIM), bf16),
            pltpu.VMEM((width, RANK), bf16),
            pltpu.VMEM((CTX_DEV // BLK, KV_HEADS, HEAD_DIM), f32),
            pltpu.VMEM((PAIRS, ROWS, HEAD_DIM), f32),
            pltpu.VMEM((PAIRS, ROWS, HEAD_DIM), f32),
            pltpu.VMEM((PAIRS, ROWS, HEAD_DIM), f32),
            pltpu.VMEM((PAIRS, ROWS, CHUNK), f32),
        ],
        compiler_params=pltpu.CompilerParams(vmem_limit_bytes=36 * 2**20),
        cost_estimate=pl.CostEstimate(
            flops=2 * macs, bytes_accessed=12 * 2**20, transcendentals=CTX_DEV * HEADS * Q_TOK
        ),
        name="attend",
    )(length, *[
        pltpu.with_memory_space_constraint(x, pltpu.HBM)
        for x in (latents.T, codes, jnp.asarray(rotary_table()), scales.T, queries, new_keys, new_values, key_factor)
    ])


def merge(a, b):
    top = jnp.maximum(a[1], b[1])
    weight_a, weight_b = (jnp.exp2((x[1] - top) * EXP2_SCALE) for x in (a, b))
    numer = a[0] * weight_a + b[0] * weight_b
    return (numer / (a[2] * weight_a + b[2] * weight_b)).astype(jnp.bfloat16)


def other_core(x):
    return lax.ppermute(x, "kv", [(0, 1), (1, 0)])


AXES = {"z": 16, "y": 4, "x": 1}
SIDE = 4
WEIGHT_AXIS = ("x", "y")
FIRST_AXIS = ("y", "z")
SECOND_AXIS = ("z", "x")
SHIFTS = (1, -1, 2)
FIRST_SHIFTS = SECOND_SHIFTS = OUT_SHIFTS = (2, 1, -1)


def coordinate(chip, axis):
    return chip // AXES[axis] % SIDE


def shifted(x, axes, shift):
    moves = []
    for chip in range(SIDE**3):
        for core, axis in enumerate(axes):
            at = coordinate(chip, axis)
            target = chip + ((at + shift) % SIDE - at) * AXES[axis]
            moves.append((chip * 2 + core, target * 2 + core))
    return lax.ppermute(x, ("group", "kv"), moves)


def gathered(x, axes):
    return jnp.concatenate([x] + [shifted(x, axes, shift) for shift in SHIFTS], axis=0)


def assemble_kernel(*refs):
    *pieces, out_ref, whole = refs
    chip, core = lax.axis_index("group"), lax.axis_index("kv")

    def place(axes, at_core, shift):
        value = jnp.int32(0)
        for c, axis in enumerate(axes):
            at = lax.rem(lax.div(chip, AXES[axis]) + (shift + SIDE), SIDE) * AXES[axis]
            value = jnp.where(at_core == c, at, value)
        return value

    for at_core, refs in ((core, pieces[:SIDE]), (1 - core, pieces[SIDE:])):
        for ref, d in zip(refs, (0,) + OUT_SHIFTS):
            for i, e in enumerate((0,) + SECOND_SHIFTS):
                for j, f in enumerate((0,) + FIRST_SHIFTS):
                    request = (
                        place(WEIGHT_AXIS, at_core, d)
                        + place(FIRST_AXIS, at_core, -f)
                        + place(SECOND_AXIS, at_core, -e)
                    )
                    row = (i * SIDE + j) * Q_TOK
                    at = pl.ds(pl.multiple_of(request * Q_TOK, Q_TOK), Q_TOK)
                    block = ref[row : row + Q_TOK, :]
                    whole[at, :] = block if at_core is core else whole[at, :] + block
    half = out_ref.shape[0]
    out_ref[...] = whole[pl.ds(pl.multiple_of(core * half, half), half), :]


def assemble(own, other):
    vmem = pl.BlockSpec(memory_space=pltpu.VMEM)
    rows, columns = SIDE * own[0].shape[0], own[0].shape[1]
    return pl.pallas_call(
        assemble_kernel,
        out_shape=jax.ShapeDtypeStruct((rows // 2, columns), jnp.float32),
        in_specs=[vmem] * 8,
        out_specs=vmem,
        scratch_shapes=[pltpu.VMEM((rows, columns), jnp.float32)],
        compiler_params=pltpu.CompilerParams(vmem_limit_bytes=4 * 2**20),
        name="assemble",
    )(*own, *other)


def body(lengths, latents, codes, scales, queries, new_keys, new_values, key_factor, out_weight):
    cut = out_weight.shape[0] // 16
    before, after = (shifted(out_weight, WEIGHT_AXIS, shift) for shift in SHIFTS[:2])
    mine, send = attend(
        lengths, latents[0], codes[0], scales[0], queries[0], new_keys[0], new_values[0], key_factor
    )
    attended = merge(mine, [other_core(part) for part in send])
    before, after = lax.optimization_barrier((before, after))
    half = out_weight.shape[0] // 2
    far = [
        shifted(before[:cut], WEIGHT_AXIS, 1),
        shifted(before[cut:half], WEIGHT_AXIS, 1),
        shifted(after[half:], WEIGHT_AXIS, -1),
    ]
    blocks = [attended[None]] + [shifted(attended[None], FIRST_AXIS, shift) for shift in FIRST_SHIFTS]
    blocks[1], far[0] = lax.optimization_barrier((blocks[1], far[0]))
    near = jnp.concatenate(blocks, axis=0)
    rows = jnp.concatenate([near] + [shifted(near, SECOND_AXIS, shift) for shift in SECOND_SHIFTS], axis=0)
    rows = rows.reshape(SIDE * SIDE * Q_TOK, HEADS // 2 * HEAD_DIM)
    distant = dot(rows[:, :cut], far[0]) + dot(rows[:, cut:half], far[1]) + dot(rows[:, half:], far[2])
    distant = shifted(distant, WEIGHT_AXIS, -2)
    pieces = [shifted(dot(rows, w), WEIGHT_AXIS, -shift) for w, shift in zip((before, after), SHIFTS)]
    pieces = [dot(rows, out_weight), distant, *pieces]
    return assemble(pieces, [other_core(p) for p in pieces])


def solution(mesh):
    placed = (
        P("group"),
        P("group", "kv", None),
        P("group", "kv", None),
        P("group", "kv", None),
        P("group", None, None),
        P("group", None, None),
        P("group", None, None),
        P(),
        P("kv", "group"),
    )
    return jax.shard_map(
        body, mesh=mesh, in_specs=placed, out_specs=P("kv", "group"), check_vma=False
    )
```

```python
import functools

import jax
import jax.numpy as jnp
import numpy as np
from jax import lax
from jax.experimental import pallas as pl
from jax.experimental.pallas import tpu as pltpu
from jax.sharding import PartitionSpec as P

HEADS = 64
KV_HEADS = 8
HEAD_DIM = 128
HALF = HEAD_DIM // 2
RANK = 160
BLK = 256
CTX_DEV = 4096
Q_TOK = 8
PAIRS = KV_HEADS // 2
ROWS = 2 * (HEADS // KV_HEADS) * Q_TOK
CHUNK = 2048
N_CHUNKS = CTX_DEV // CHUNK
ROPE_BASE = 500000.0
NEG_FILL = -1e30
EXP2_SCALE = float(HEAD_DIM**-0.5 * np.log2(np.e))


def rotary_table():
    freq = np.float32(ROPE_BASE) ** (-(np.arange(HALF, dtype=np.float32) * 2.0) / HEAD_DIM)
    angles = np.arange(2 * CTX_DEV, dtype=np.float32)[None, :] * freq.astype(np.float32)[:, None]
    angles = angles.reshape(HALF, 2, CTX_DEV).astype(np.float64)
    return np.stack([np.cos(angles), np.sin(angles)]).transpose(2, 0, 1, 3).astype(np.float32)


STRIP = 16


def strip_order():
    starts = [
        head * HEAD_DIM + half * HALF + m * STRIP
        for m in range(HALF // STRIP)
        for head in range(2)
        for half in range(2)
    ]
    return np.concatenate([np.arange(a, a + STRIP) for a in starts])


def dot(a, b):
    return jnp.dot(a, b, preferred_element_type=jnp.float32)


def own_blocks(x):
    return jnp.concatenate([x[: ROWS // 2, :HEAD_DIM], x[ROWS // 2 :, HEAD_DIM:]], axis=0)


def attend_kernel(
    length_ref, lat_hbm, code_hbm, table_hbm, scale_hbm, q_hbm, nk_hbm, nv_hbm, kf_hbm,
    mine_ref, send_ref,
    lat_buf, code_buf, table_buf, scale_buf, q_buf, nk_buf, nv_buf, kf_buf,
    lat_sem, code_sem, table_sem, small_sem,
    qc, wt, scale_rows, peak, total, numer, scores,
):
    f32, bf16 = jnp.float32, jnp.bfloat16
    kv_at = lax.axis_index("kv")
    valid = jnp.clip(length_ref[0] - kv_at * CTX_DEV, 0, CTX_DEV)
    chunks = lax.div(valid + (CHUNK - 1), CHUNK)

    small = [
        pltpu.make_async_copy(src, dst, small_sem.at[i])
        for i, (src, dst) in enumerate(
            ((kf_hbm, kf_buf), (q_hbm, q_buf), (nk_hbm, nk_buf), (nv_hbm, nv_buf), (scale_hbm, scale_buf))
        )
    ]
    for copy in small:
        copy.start()

    def at(c):
        return pl.ds(pl.multiple_of(c * CHUNK, CHUNK), CHUNK)

    def key_copies(c):
        return (
            pltpu.make_async_copy(lat_hbm.at[:, at(c)], lat_buf.at[:, at(c)], lat_sem.at[c]),
            pltpu.make_async_copy(table_hbm.at[kv_at, :, :, at(c)], table_buf.at[:, :, at(c)], table_sem.at[c]),
        )

    def code_copy(c):
        return pltpu.make_async_copy(code_hbm.at[at(c)], code_buf.at[at(c)], code_sem.at[c])

    @pl.loop(0, chunks)
    def _(c):
        for copy in key_copies(c):
            copy.start()

    @pl.loop(0, chunks)
    def _(c):
        code_copy(c).start()

    for copy in small:
        copy.wait()
    scales = scale_buf[...].astype(f32)
    for b in range(CTX_DEV // BLK):
        scale_rows[b] = jnp.broadcast_to(scales[:, b : b + 1], (KV_HEADS, HEAD_DIM))
    row_tok = lax.rem(lax.broadcasted_iota(jnp.int32, (ROWS, HEAD_DIM), 0), Q_TOK)
    lane = lax.broadcasted_iota(jnp.int32, (ROWS, HEAD_DIM), 1)
    causal = jnp.logical_and(lane <= row_tok, kv_at == 0)
    queries = q_buf[...].astype(f32)
    new_keys = nk_buf[...].astype(f32)
    new_values = nv_buf[...].astype(f32)
    pad = jnp.zeros((HEAD_DIM - Q_TOK, 2 * HEAD_DIM), f32)
    groups = HEADS // KV_HEADS
    blank = jnp.zeros((ROWS // 2, HEAD_DIM), f32)

    def head_rows(k):
        return jnp.concatenate(
            [queries[:, (k * groups + g) * HEAD_DIM : (k * groups + g + 1) * HEAD_DIM] for g in range(groups)],
            axis=0,
        )

    order = strip_order()
    source = lax.broadcasted_iota(jnp.int32, (2 * HEAD_DIM, 2 * HEAD_DIM), 0)
    target = lax.broadcasted_iota(jnp.int32, (2 * HEAD_DIM, 2 * HEAD_DIM), 1)
    strip, inside = lax.div(target, STRIP), lax.rem(target, STRIP)
    wanted = (
        lax.rem(lax.div(strip, 2), 2) * HEAD_DIM + lax.rem(strip, 2) * HALF + lax.div(strip, 4) * STRIP + inside
    )
    arrange = jnp.where(source == wanted, 1.0, 0.0).astype(bf16)

    for j in range(PAIRS):
        columns = slice(2 * j * HEAD_DIM, (2 * j + 2) * HEAD_DIM)
        plain = jnp.concatenate(
            [
                jnp.concatenate([head_rows(2 * j), blank], axis=1),
                jnp.concatenate([blank, head_rows(2 * j + 1)], axis=1),
            ],
            axis=0,
        ).astype(bf16)
        qc[j] = dot(plain, arrange).astype(bf16)
        turned = kf_buf[:, columns].astype(f32).T
        wt[columns, :] = jnp.concatenate(
            [turned[a : a + STRIP] for a in order[::STRIP]], axis=0
        ).astype(bf16)
        fresh_keys = jnp.concatenate([new_keys[:, columns], pad], axis=0).astype(bf16)
        fresh_values = jnp.concatenate([new_values[:, columns], pad], axis=0).astype(bf16)
        s = lax.dot_general(plain, fresh_keys, (((1,), (1,)), ((), ())), preferred_element_type=f32)
        s = jnp.where(causal, s, NEG_FILL)
        top = jnp.broadcast_to(jnp.max(s, axis=1, keepdims=True), s.shape)
        weights = jnp.where(causal, jnp.exp2((s - top) * EXP2_SCALE), 0.0)
        peak[j] = top
        total[j] = weights
        numer[j] = own_blocks(dot(weights.astype(bf16), fresh_values))

    def make_keys(c):
        for copy in key_copies(c):
            copy.wait()
        lat = lat_buf[:, at(c)]
        every = []
        for j in range(PAIRS):
            columns = slice(2 * j * HEAD_DIM, (2 * j + 2) * HEAD_DIM)
            cos, sin = table_buf[0, :, at(c)], table_buf[1, :, at(c)]
            pre = dot(wt[columns, :], lat)
            keys = []
            for m in range(HALF // STRIP):
                here = slice(m * STRIP, (m + 1) * STRIP)
                for i in range(2):
                    at_lo = (4 * m + 2 * i) * STRIP
                    lo, hi = pre[at_lo : at_lo + STRIP], pre[at_lo + STRIP : at_lo + 2 * STRIP]
                    keys.append((lo * cos[here] - hi * sin[here]).astype(bf16))
                    keys.append((hi * cos[here] + lo * sin[here]).astype(bf16))
            every.append(jnp.concatenate(keys, axis=0))
        return every

    def make_scores(c, keys):
        position = c * CHUNK + lax.broadcasted_iota(jnp.int32, (1, CHUNK), 1)
        hide = jnp.where(position < valid, 0.0, NEG_FILL)
        for j in range(PAIRS):
            scores[j] = dot(qc[j], keys[j]) + hide

    def weigh(j):
        s = scores[j]
        old = peak[j]
        new = jnp.maximum(old, jnp.max(s, axis=1, keepdims=True))
        shrink = jnp.exp2((old - new) * EXP2_SCALE)
        weights = [
            jnp.exp2((s[:, i : i + HEAD_DIM] - new) * EXP2_SCALE) for i in range(0, CHUNK, HEAD_DIM)
        ]
        peak[j] = new
        total[j] = total[j] * shrink + functools.reduce(jnp.add, weights)
        return shrink, [w.astype(bf16) for w in weights]

    def add_values(c, j, shrink, rounded):
        columns = slice(2 * j * HEAD_DIM, (2 * j + 2) * HEAD_DIM)
        result = numer[j] * shrink
        for b in range(CHUNK // BLK):
            per = BLK // HEAD_DIM
            w = jnp.concatenate(rounded[b * per : (b + 1) * per], axis=1)
            v = code_buf[pl.ds(pl.multiple_of(c * CHUNK + b * BLK, BLK), BLK), columns]
            part = own_blocks(dot(w, v))
            block = c * (CHUNK // BLK) + b
            factor = jnp.concatenate(
                [
                    jnp.broadcast_to(scale_rows[block, 2 * j + i : 2 * j + i + 1, :], (ROWS // 2, HEAD_DIM))
                    for i in range(2)
                ],
                axis=0,
            )
            result = result + part * factor
        numer[j] = result

    @pl.when(chunks > 0)
    def _():
        make_scores(0, make_keys(0))

    @pl.loop(0, chunks - 1)
    def _(c):
        code_copy(c).wait()
        keys = make_keys(c + 1)
        weighed = [weigh(j) for j in range(PAIRS)]
        make_scores(c + 1, keys)
        for j in range(PAIRS):
            add_values(c, j, *weighed[j])

    @pl.when(chunks > 0)
    def _():
        code_copy(chunks - 1).wait()
        weighed = [weigh(j) for j in range(PAIRS)]
        for j in range(PAIRS):
            add_values(chunks - 1, j, *weighed[j])

    for j in range(PAIRS):
        total[j] = jnp.broadcast_to(jnp.sum(total[j], axis=1, keepdims=True), (ROWS, HEAD_DIM))
    half = PAIRS // 2
    for ref, first in ((mine_ref, kv_at * half), (send_ref, (1 - kv_at) * half)):
        for part, state in enumerate((numer, peak, total)):
            for i in range(half):
                whole = state[first + i]
                for h in range(ROWS // Q_TOK):
                    column = (i * (ROWS // Q_TOK) + h) * HEAD_DIM
                    ref[part, :, column : column + HEAD_DIM] = whole[h * Q_TOK : (h + 1) * Q_TOK]


def attend(length, latents, codes, scales, queries, new_keys, new_values, key_factor):
    f32, bf16 = jnp.float32, jnp.bfloat16
    vmem = pl.BlockSpec(memory_space=pltpu.VMEM)
    hbm = pl.BlockSpec(memory_space=pltpu.HBM)
    shape = jax.ShapeDtypeStruct((3, Q_TOK, HEADS // 2 * HEAD_DIM), f32)
    macs = CTX_DEV * (RANK * KV_HEADS + 2 * PAIRS * ROWS * 2) * HEAD_DIM
    width = KV_HEADS * HEAD_DIM
    return pl.pallas_call(
        attend_kernel,
        out_shape=(shape, shape),
        in_specs=[pl.BlockSpec(memory_space=pltpu.SMEM)] + [hbm] * 8,
        out_specs=(vmem, vmem),
        scratch_shapes=[
            pltpu.VMEM((RANK, CTX_DEV), bf16),
            pltpu.VMEM((CTX_DEV, width), bf16),
            pltpu.VMEM((2, HALF, CTX_DEV), f32),
            pltpu.VMEM((KV_HEADS, CTX_DEV // BLK), bf16),
            pltpu.VMEM((Q_TOK, HEADS * HEAD_DIM), bf16),
            pltpu.VMEM((Q_TOK, width), bf16),
            pltpu.VMEM((Q_TOK, width), bf16),
            pltpu.VMEM((RANK, width), bf16),
            pltpu.SemaphoreType.DMA((N_CHUNKS,)),
            pltpu.SemaphoreType.DMA((N_CHUNKS,)),
            pltpu.SemaphoreType.DMA((N_CHUNKS,)),
            pltpu.SemaphoreType.DMA((5,)),
            pltpu.VMEM((PAIRS, ROWS, 2 * HEAD_DIM), bf16),
            pltpu.VMEM((width, RANK), bf16),
            pltpu.VMEM((CTX_DEV // BLK, KV_HEADS, HEAD_DIM), f32),
            pltpu.VMEM((PAIRS, ROWS, HEAD_DIM), f32),
            pltpu.VMEM((PAIRS, ROWS, HEAD_DIM), f32),
            pltpu.VMEM((PAIRS, ROWS, HEAD_DIM), f32),
            pltpu.VMEM((PAIRS, ROWS, CHUNK), f32),
        ],
        compiler_params=pltpu.CompilerParams(vmem_limit_bytes=36 * 2**20),
        cost_estimate=pl.CostEstimate(
            flops=2 * macs, bytes_accessed=12 * 2**20, transcendentals=CTX_DEV * HEADS * Q_TOK
        ),
        name="attend",
    )(length, *[
        pltpu.with_memory_space_constraint(x, pltpu.HBM)
        for x in (latents.T, codes, jnp.asarray(rotary_table()), scales.T, queries, new_keys, new_values, key_factor)
    ])


def merge(a, b):
    top = jnp.maximum(a[1], b[1])
    weight_a, weight_b = (jnp.exp2((x[1] - top) * EXP2_SCALE) for x in (a, b))
    numer = a[0] * weight_a + b[0] * weight_b
    return (numer / (a[2] * weight_a + b[2] * weight_b)).astype(jnp.bfloat16)


def other_core(x):
    return lax.ppermute(x, "kv", [(0, 1), (1, 0)])


AXES = {"z": 16, "y": 4, "x": 1}
SIDE = 4
WEIGHT_AXIS = ("y", "z")
FIRST_AXIS = ("z", "x")
SECOND_AXIS = ("x", "y")
SHIFTS = (1, -1, 2)
FIRST_SHIFTS = SECOND_SHIFTS = OUT_SHIFTS = (2, 1, -1)


def coordinate(chip, axis):
    return chip // AXES[axis] % SIDE


def shifted(x, axes, shift):
    moves = []
    for chip in range(SIDE**3):
        for core, axis in enumerate(axes):
            at = coordinate(chip, axis)
            target = chip + ((at + shift) % SIDE - at) * AXES[axis]
            moves.append((chip * 2 + core, target * 2 + core))
    return lax.ppermute(x, ("group", "kv"), moves)


def gathered(x, axes):
    return jnp.concatenate([x] + [shifted(x, axes, shift) for shift in SHIFTS], axis=0)


def assemble_kernel(*refs):
    *pieces, out_ref, whole = refs
    chip, core = lax.axis_index("group"), lax.axis_index("kv")

    def place(axes, at_core, shift):
        value = jnp.int32(0)
        for c, axis in enumerate(axes):
            at = lax.rem(lax.div(chip, AXES[axis]) + (shift + SIDE), SIDE) * AXES[axis]
            value = jnp.where(at_core == c, at, value)
        return value

    for at_core, refs in ((core, pieces[:SIDE]), (1 - core, pieces[SIDE:])):
        for ref, d in zip(refs, (0,) + OUT_SHIFTS):
            for i, e in enumerate((0,) + SECOND_SHIFTS):
                for j, f in enumerate((0,) + FIRST_SHIFTS):
                    request = (
                        place(WEIGHT_AXIS, at_core, d)
                        + place(FIRST_AXIS, at_core, -f)
                        + place(SECOND_AXIS, at_core, -e)
                    )
                    row = (i * SIDE + j) * Q_TOK
                    at = pl.ds(pl.multiple_of(request * Q_TOK, Q_TOK), Q_TOK)
                    block = ref[row : row + Q_TOK, :]
                    whole[at, :] = block if at_core is core else whole[at, :] + block
    half = out_ref.shape[0]
    out_ref[...] = whole[pl.ds(pl.multiple_of(core * half, half), half), :]


def assemble(own, other):
    vmem = pl.BlockSpec(memory_space=pltpu.VMEM)
    rows, columns = SIDE * own[0].shape[0], own[0].shape[1]
    return pl.pallas_call(
        assemble_kernel,
        out_shape=jax.ShapeDtypeStruct((rows // 2, columns), jnp.float32),
        in_specs=[vmem] * 8,
        out_specs=vmem,
        scratch_shapes=[pltpu.VMEM((rows, columns), jnp.float32)],
        compiler_params=pltpu.CompilerParams(vmem_limit_bytes=4 * 2**20),
        name="assemble",
    )(*own, *other)


def body(lengths, latents, codes, scales, queries, new_keys, new_values, key_factor, out_weight):
    cut = out_weight.shape[0] // 16
    before, after = (shifted(out_weight, WEIGHT_AXIS, shift) for shift in SHIFTS[:2])
    mine, send = attend(
        lengths, latents[0], codes[0], scales[0], queries[0], new_keys[0], new_values[0], key_factor
    )
    attended = merge(mine, [other_core(part) for part in send])
    before, after = lax.optimization_barrier((before, after))
    half = out_weight.shape[0] // 2
    far = [
        shifted(before[:cut], WEIGHT_AXIS, 1),
        shifted(before[cut:half], WEIGHT_AXIS, 1),
        shifted(after[half:], WEIGHT_AXIS, -1),
    ]
    blocks = [attended[None]] + [shifted(attended[None], FIRST_AXIS, shift) for shift in FIRST_SHIFTS]
    blocks[1], far[0] = lax.optimization_barrier((blocks[1], far[0]))
    near = jnp.concatenate(blocks, axis=0)
    rows = jnp.concatenate([near] + [shifted(near, SECOND_AXIS, shift) for shift in SECOND_SHIFTS], axis=0)
    rows = rows.reshape(SIDE * SIDE * Q_TOK, HEADS // 2 * HEAD_DIM)
    distant = dot(rows[:, :cut], far[0]) + dot(rows[:, cut:half], far[1]) + dot(rows[:, half:], far[2])
    distant = shifted(distant, WEIGHT_AXIS, -2)
    pieces = [shifted(dot(rows, w), WEIGHT_AXIS, -shift) for w, shift in zip((before, after), SHIFTS)]
    pieces = [dot(rows, out_weight), distant, *pieces]
    return assemble(pieces, [other_core(p) for p in pieces])


def solution(mesh):
    placed = (
        P("group"),
        P("group", "kv", None),
        P("group", "kv", None),
        P("group", "kv", None),
        P("group", None, None),
        P("group", None, None),
        P("group", None, None),
        P(),
        P("kv", "group"),
    )
    return jax.shard_map(
        body, mesh=mesh, in_specs=placed, out_specs=P("kv", "group"), check_vma=False
    )
```

```python
import functools

import jax
import jax.numpy as jnp
import numpy as np
from jax import lax
from jax.experimental import pallas as pl
from jax.experimental.pallas import tpu as pltpu
from jax.sharding import PartitionSpec as P

HEADS = 64
KV_HEADS = 8
HEAD_DIM = 128
HALF = HEAD_DIM // 2
RANK = 160
BLK = 256
CTX_DEV = 4096
Q_TOK = 8
PAIRS = KV_HEADS // 2
ROWS = 2 * (HEADS // KV_HEADS) * Q_TOK
CHUNK = 2048
N_CHUNKS = CTX_DEV // CHUNK
ROPE_BASE = 500000.0
NEG_FILL = -1e30
EXP2_SCALE = float(HEAD_DIM**-0.5 * np.log2(np.e))


def rotary_table():
    freq = np.float32(ROPE_BASE) ** (-(np.arange(HALF, dtype=np.float32) * 2.0) / HEAD_DIM)
    angles = np.arange(2 * CTX_DEV, dtype=np.float32)[None, :] * freq.astype(np.float32)[:, None]
    angles = angles.reshape(HALF, 2, CTX_DEV).astype(np.float64)
    return np.stack([np.cos(angles), np.sin(angles)]).transpose(2, 0, 1, 3).astype(np.float32)


STRIP = 16


def strip_order():
    starts = [
        head * HEAD_DIM + half * HALF + m * STRIP
        for m in range(HALF // STRIP)
        for head in range(2)
        for half in range(2)
    ]
    return np.concatenate([np.arange(a, a + STRIP) for a in starts])


def dot(a, b):
    return jnp.dot(a, b, preferred_element_type=jnp.float32)


def own_blocks(x):
    return jnp.concatenate([x[: ROWS // 2, :HEAD_DIM], x[ROWS // 2 :, HEAD_DIM:]], axis=0)


def attend_kernel(
    length_ref, lat_hbm, code_hbm, table_hbm, scale_hbm, q_hbm, nk_hbm, nv_hbm, kf_hbm,
    mine_ref, send_ref,
    lat_buf, code_buf, table_buf, scale_buf, q_buf, nk_buf, nv_buf, kf_buf,
    lat_sem, code_sem, table_sem, small_sem,
    qc, wt, scale_rows, peak, total, numer, scores,
):
    f32, bf16 = jnp.float32, jnp.bfloat16
    kv_at = lax.axis_index("kv")
    valid = jnp.clip(length_ref[0] - kv_at * CTX_DEV, 0, CTX_DEV)
    chunks = lax.div(valid + (CHUNK - 1), CHUNK)

    small = [
        pltpu.make_async_copy(src, dst, small_sem.at[i])
        for i, (src, dst) in enumerate(
            ((kf_hbm, kf_buf), (q_hbm, q_buf), (nk_hbm, nk_buf), (nv_hbm, nv_buf), (scale_hbm, scale_buf))
        )
    ]
    for copy in small:
        copy.start()

    def at(c):
        return pl.ds(pl.multiple_of(c * CHUNK, CHUNK), CHUNK)

    def key_copies(c):
        return (
            pltpu.make_async_copy(lat_hbm.at[:, at(c)], lat_buf.at[:, at(c)], lat_sem.at[c]),
            pltpu.make_async_copy(table_hbm.at[kv_at, :, :, at(c)], table_buf.at[:, :, at(c)], table_sem.at[c]),
        )

    def code_copy(c):
        return pltpu.make_async_copy(code_hbm.at[at(c)], code_buf.at[at(c)], code_sem.at[c])

    @pl.loop(0, chunks)
    def _(c):
        for copy in key_copies(c):
            copy.start()

    @pl.loop(0, chunks)
    def _(c):
        code_copy(c).start()

    for copy in small:
        copy.wait()
    scales = scale_buf[...].astype(f32)
    for b in range(CTX_DEV // BLK):
        scale_rows[b] = jnp.broadcast_to(scales[:, b : b + 1], (KV_HEADS, HEAD_DIM))
    row_tok = lax.rem(lax.broadcasted_iota(jnp.int32, (ROWS, HEAD_DIM), 0), Q_TOK)
    lane = lax.broadcasted_iota(jnp.int32, (ROWS, HEAD_DIM), 1)
    causal = jnp.logical_and(lane <= row_tok, kv_at == 0)
    queries = q_buf[...].astype(f32)
    new_keys = nk_buf[...].astype(f32)
    new_values = nv_buf[...].astype(f32)
    pad = jnp.zeros((HEAD_DIM - Q_TOK, 2 * HEAD_DIM), f32)
    groups = HEADS // KV_HEADS
    blank = jnp.zeros((ROWS // 2, HEAD_DIM), f32)

    def head_rows(k):
        return jnp.concatenate(
            [queries[:, (k * groups + g) * HEAD_DIM : (k * groups + g + 1) * HEAD_DIM] for g in range(groups)],
            axis=0,
        )

    order = strip_order()
    source = lax.broadcasted_iota(jnp.int32, (2 * HEAD_DIM, 2 * HEAD_DIM), 0)
    target = lax.broadcasted_iota(jnp.int32, (2 * HEAD_DIM, 2 * HEAD_DIM), 1)
    strip, inside = lax.div(target, STRIP), lax.rem(target, STRIP)
    wanted = (
        lax.rem(lax.div(strip, 2), 2) * HEAD_DIM + lax.rem(strip, 2) * HALF + lax.div(strip, 4) * STRIP + inside
    )
    arrange = jnp.where(source == wanted, 1.0, 0.0).astype(bf16)

    for j in range(PAIRS):
        columns = slice(2 * j * HEAD_DIM, (2 * j + 2) * HEAD_DIM)
        plain = jnp.concatenate(
            [
                jnp.concatenate([head_rows(2 * j), blank], axis=1),
                jnp.concatenate([blank, head_rows(2 * j + 1)], axis=1),
            ],
            axis=0,
        ).astype(bf16)
        qc[j] = dot(plain, arrange).astype(bf16)
        turned = kf_buf[:, columns].astype(f32).T
        wt[columns, :] = jnp.concatenate(
            [turned[a : a + STRIP] for a in order[::STRIP]], axis=0
        ).astype(bf16)
        fresh_keys = jnp.concatenate([new_keys[:, columns], pad], axis=0).astype(bf16)
        fresh_values = jnp.concatenate([new_values[:, columns], pad], axis=0).astype(bf16)
        s = lax.dot_general(plain, fresh_keys, (((1,), (1,)), ((), ())), preferred_element_type=f32)
        s = jnp.where(causal, s, NEG_FILL)
        top = jnp.broadcast_to(jnp.max(s, axis=1, keepdims=True), s.shape)
        weights = jnp.where(causal, jnp.exp2((s - top) * EXP2_SCALE), 0.0)
        peak[j] = top
        total[j] = weights
        numer[j] = own_blocks(dot(weights.astype(bf16), fresh_values))

    def make_keys(c):
        for copy in key_copies(c):
            copy.wait()
        lat = lat_buf[:, at(c)]
        every = []
        for j in range(PAIRS):
            columns = slice(2 * j * HEAD_DIM, (2 * j + 2) * HEAD_DIM)
            cos, sin = table_buf[0, :, at(c)], table_buf[1, :, at(c)]
            pre = dot(wt[columns, :], lat)
            keys = []
            for m in range(HALF // STRIP):
                here = slice(m * STRIP, (m + 1) * STRIP)
                for i in range(2):
                    at_lo = (4 * m + 2 * i) * STRIP
                    lo, hi = pre[at_lo : at_lo + STRIP], pre[at_lo + STRIP : at_lo + 2 * STRIP]
                    keys.append((lo * cos[here] - hi * sin[here]).astype(bf16))
                    keys.append((hi * cos[here] + lo * sin[here]).astype(bf16))
            every.append(jnp.concatenate(keys, axis=0))
        return every

    def make_scores(c, keys):
        position = c * CHUNK + lax.broadcasted_iota(jnp.int32, (1, CHUNK), 1)
        hide = jnp.where(position < valid, 0.0, NEG_FILL)
        for j in range(PAIRS):
            scores[j] = dot(qc[j], keys[j]) + hide

    def weigh(j):
        s = scores[j]
        old = peak[j]
        new = jnp.maximum(old, jnp.max(s, axis=1, keepdims=True))
        shrink = jnp.exp2((old - new) * EXP2_SCALE)
        weights = [
            jnp.exp2((s[:, i : i + HEAD_DIM] - new) * EXP2_SCALE) for i in range(0, CHUNK, HEAD_DIM)
        ]
        peak[j] = new
        total[j] = total[j] * shrink + functools.reduce(jnp.add, weights)
        return shrink, [w.astype(bf16) for w in weights]

    def add_values(c, j, shrink, rounded):
        columns = slice(2 * j * HEAD_DIM, (2 * j + 2) * HEAD_DIM)
        result = numer[j] * shrink
        for b in range(CHUNK // BLK):
            per = BLK // HEAD_DIM
            w = jnp.concatenate(rounded[b * per : (b + 1) * per], axis=1)
            v = code_buf[pl.ds(pl.multiple_of(c * CHUNK + b * BLK, BLK), BLK), columns]
            part = own_blocks(dot(w, v))
            block = c * (CHUNK // BLK) + b
            factor = jnp.concatenate(
                [
                    jnp.broadcast_to(scale_rows[block, 2 * j + i : 2 * j + i + 1, :], (ROWS // 2, HEAD_DIM))
                    for i in range(2)
                ],
                axis=0,
            )
            result = result + part * factor
        numer[j] = result

    @pl.when(chunks > 0)
    def _():
        make_scores(0, make_keys(0))

    @pl.loop(0, chunks - 1)
    def _(c):
        code_copy(c).wait()
        keys = make_keys(c + 1)
        weighed = [weigh(j) for j in range(PAIRS)]
        make_scores(c + 1, keys)
        for j in range(PAIRS):
            add_values(c, j, *weighed[j])

    @pl.when(chunks > 0)
    def _():
        code_copy(chunks - 1).wait()
        weighed = [weigh(j) for j in range(PAIRS)]
        for j in range(PAIRS):
            add_values(chunks - 1, j, *weighed[j])

    for j in range(PAIRS):
        total[j] = jnp.broadcast_to(jnp.sum(total[j], axis=1, keepdims=True), (ROWS, HEAD_DIM))
    half = PAIRS // 2
    for ref, first in ((mine_ref, kv_at * half), (send_ref, (1 - kv_at) * half)):
        for part, state in enumerate((numer, peak, total)):
            for i in range(half):
                whole = state[first + i]
                for h in range(ROWS // Q_TOK):
                    column = (i * (ROWS // Q_TOK) + h) * HEAD_DIM
                    ref[part, :, column : column + HEAD_DIM] = whole[h * Q_TOK : (h + 1) * Q_TOK]


def attend(length, latents, codes, scales, queries, new_keys, new_values, key_factor):
    f32, bf16 = jnp.float32, jnp.bfloat16
    vmem = pl.BlockSpec(memory_space=pltpu.VMEM)
    hbm = pl.BlockSpec(memory_space=pltpu.HBM)
    shape = jax.ShapeDtypeStruct((3, Q_TOK, HEADS // 2 * HEAD_DIM), f32)
    macs = CTX_DEV * (RANK * KV_HEADS + 2 * PAIRS * ROWS * 2) * HEAD_DIM
    width = KV_HEADS * HEAD_DIM
    return pl.pallas_call(
        attend_kernel,
        out_shape=(shape, shape),
        in_specs=[pl.BlockSpec(memory_space=pltpu.SMEM)] + [hbm] * 8,
        out_specs=(vmem, vmem),
        scratch_shapes=[
            pltpu.VMEM((RANK, CTX_DEV), bf16),
            pltpu.VMEM((CTX_DEV, width), bf16),
            pltpu.VMEM((2, HALF, CTX_DEV), f32),
            pltpu.VMEM((KV_HEADS, CTX_DEV // BLK), bf16),
            pltpu.VMEM((Q_TOK, HEADS * HEAD_DIM), bf16),
            pltpu.VMEM((Q_TOK, width), bf16),
            pltpu.VMEM((Q_TOK, width), bf16),
            pltpu.VMEM((RANK, width), bf16),
            pltpu.SemaphoreType.DMA((N_CHUNKS,)),
            pltpu.SemaphoreType.DMA((N_CHUNKS,)),
            pltpu.SemaphoreType.DMA((N_CHUNKS,)),
            pltpu.SemaphoreType.DMA((5,)),
            pltpu.VMEM((PAIRS, ROWS, 2 * HEAD_DIM), bf16),
            pltpu.VMEM((width, RANK), bf16),
            pltpu.VMEM((CTX_DEV // BLK, KV_HEADS, HEAD_DIM), f32),
            pltpu.VMEM((PAIRS, ROWS, HEAD_DIM), f32),
            pltpu.VMEM((PAIRS, ROWS, HEAD_DIM), f32),
            pltpu.VMEM((PAIRS, ROWS, HEAD_DIM), f32),
            pltpu.VMEM((PAIRS, ROWS, CHUNK), f32),
        ],
        compiler_params=pltpu.CompilerParams(vmem_limit_bytes=36 * 2**20),
        cost_estimate=pl.CostEstimate(
            flops=2 * macs, bytes_accessed=12 * 2**20, transcendentals=CTX_DEV * HEADS * Q_TOK
        ),
        name="attend",
    )(length, *[
        pltpu.with_memory_space_constraint(x, pltpu.HBM)
        for x in (latents.T, codes, jnp.asarray(rotary_table()), scales.T, queries, new_keys, new_values, key_factor)
    ])


def merge(a, b):
    top = jnp.maximum(a[1], b[1])
    weight_a, weight_b = (jnp.exp2((x[1] - top) * EXP2_SCALE) for x in (a, b))
    numer = a[0] * weight_a + b[0] * weight_b
    return (numer / (a[2] * weight_a + b[2] * weight_b)).astype(jnp.bfloat16)


def other_core(x):
    return lax.ppermute(x, "kv", [(0, 1), (1, 0)])


AXES = {"z": 16, "y": 4, "x": 1}
SIDE = 4
WEIGHT_AXIS = ("y", "z")
FIRST_AXIS = ("z", "x")
SECOND_AXIS = ("x", "y")
SHIFTS = (1, -1, 2)
FIRST_SHIFTS = SECOND_SHIFTS = OUT_SHIFTS = (2, 1, -1)


def coordinate(chip, axis):
    return chip // AXES[axis] % SIDE


def shifted(x, axes, shift):
    moves = []
    for chip in range(SIDE**3):
        for core, axis in enumerate(axes):
            at = coordinate(chip, axis)
            target = chip + ((at + shift) % SIDE - at) * AXES[axis]
            moves.append((chip * 2 + core, target * 2 + core))
    return lax.ppermute(x, ("group", "kv"), moves)


def gathered(x, axes):
    return jnp.concatenate([x] + [shifted(x, axes, shift) for shift in SHIFTS], axis=0)


def assemble_kernel(*refs):
    *pieces, out_ref, whole = refs
    chip, core = lax.axis_index("group"), lax.axis_index("kv")

    def place(axes, at_core, shift):
        value = jnp.int32(0)
        for c, axis in enumerate(axes):
            at = lax.rem(lax.div(chip, AXES[axis]) + (shift + SIDE), SIDE) * AXES[axis]
            value = jnp.where(at_core == c, at, value)
        return value

    for at_core, refs in ((core, pieces[:SIDE]), (1 - core, pieces[SIDE:])):
        for ref, d in zip(refs, (0,) + OUT_SHIFTS):
            for i, e in enumerate((0,) + SECOND_SHIFTS):
                for j, f in enumerate((0,) + FIRST_SHIFTS):
                    request = (
                        place(WEIGHT_AXIS, at_core, d)
                        + place(FIRST_AXIS, at_core, -f)
                        + place(SECOND_AXIS, at_core, -e)
                    )
                    row = (i * SIDE + j) * Q_TOK
                    at = pl.ds(pl.multiple_of(request * Q_TOK, Q_TOK), Q_TOK)
                    block = ref[row : row + Q_TOK, :]
                    whole[at, :] = block if at_core is core else whole[at, :] + block
    half = out_ref.shape[0]
    out_ref[...] = whole[pl.ds(pl.multiple_of(core * half, half), half), :]


def assemble(own, other):
    vmem = pl.BlockSpec(memory_space=pltpu.VMEM)
    rows, columns = SIDE * own[0].shape[0], own[0].shape[1]
    return pl.pallas_call(
        assemble_kernel,
        out_shape=jax.ShapeDtypeStruct((rows // 2, columns), jnp.float32),
        in_specs=[vmem] * 8,
        out_specs=vmem,
        scratch_shapes=[pltpu.VMEM((rows, columns), jnp.float32)],
        compiler_params=pltpu.CompilerParams(vmem_limit_bytes=4 * 2**20),
        name="assemble",
    )(*own, *other)


def body(lengths, latents, codes, scales, queries, new_keys, new_values, key_factor, out_weight):
    cut = out_weight.shape[0] // 16
    before, after = (shifted(out_weight, WEIGHT_AXIS, shift) for shift in SHIFTS[:2])
    mine, send = attend(
        lengths, latents[0], codes[0], scales[0], queries[0], new_keys[0], new_values[0], key_factor
    )
    attended = merge(mine, [other_core(part) for part in send])
    before, after = lax.optimization_barrier((before, after))
    half = out_weight.shape[0] // 2
    far = [
        shifted(before[:cut], WEIGHT_AXIS, 1),
        shifted(after[cut:half], WEIGHT_AXIS, -1),
        shifted(before[half:], WEIGHT_AXIS, 1),
    ]
    blocks = [attended[None]] + [shifted(attended[None], FIRST_AXIS, shift) for shift in FIRST_SHIFTS]
    blocks[1], far[0] = lax.optimization_barrier((blocks[1], far[0]))
    near = jnp.concatenate(blocks, axis=0)
    rows = jnp.concatenate([near] + [shifted(near, SECOND_AXIS, shift) for shift in SECOND_SHIFTS], axis=0)
    rows = rows.reshape(SIDE * SIDE * Q_TOK, HEADS // 2 * HEAD_DIM)
    distant = dot(rows[:, :cut], far[0]) + dot(rows[:, cut:half], far[1]) + dot(rows[:, half:], far[2])
    distant = shifted(distant, WEIGHT_AXIS, -2)
    pieces = [shifted(dot(rows, w), WEIGHT_AXIS, -shift) for w, shift in zip((before, after), SHIFTS)]
    pieces = [dot(rows, out_weight), distant, *pieces]
    return assemble(pieces, [other_core(p) for p in pieces])


def solution(mesh):
    placed = (
        P("group"),
        P("group", "kv", None),
        P("group", "kv", None),
        P("group", "kv", None),
        P("group", None, None),
        P("group", None, None),
        P("group", None, None),
        P(),
        P("kv", "group"),
    )
    return jax.shard_map(
        body, mesh=mesh, in_specs=placed, out_specs=P("kv", "group"), check_vma=False
    )
```

```python
import functools

import jax
import jax.numpy as jnp
import numpy as np
from jax import lax
from jax.experimental import pallas as pl
from jax.experimental.pallas import tpu as pltpu
from jax.sharding import PartitionSpec as P

HEADS = 64
KV_HEADS = 8
HEAD_DIM = 128
HALF = HEAD_DIM // 2
RANK = 160
BLK = 256
CTX_DEV = 4096
Q_TOK = 8
PAIRS = KV_HEADS // 2
ROWS = 2 * (HEADS // KV_HEADS) * Q_TOK
CHUNK = 2048
N_CHUNKS = CTX_DEV // CHUNK
ROPE_BASE = 500000.0
NEG_FILL = -1e30
EXP2_SCALE = float(HEAD_DIM**-0.5 * np.log2(np.e))


def rotary_table():
    freq = np.float32(ROPE_BASE) ** (-(np.arange(HALF, dtype=np.float32) * 2.0) / HEAD_DIM)
    angles = np.arange(2 * CTX_DEV, dtype=np.float32)[None, :] * freq.astype(np.float32)[:, None]
    angles = angles.reshape(HALF, 2, CTX_DEV).astype(np.float64)
    return np.stack([np.cos(angles), np.sin(angles)]).transpose(2, 0, 1, 3).astype(np.float32)


STRIP = 16


def strip_order():
    starts = [
        head * HEAD_DIM + half * HALF + m * STRIP
        for m in range(HALF // STRIP)
        for head in range(2)
        for half in range(2)
    ]
    return np.concatenate([np.arange(a, a + STRIP) for a in starts])


def dot(a, b):
    return jnp.dot(a, b, preferred_element_type=jnp.float32)


def own_blocks(x):
    return jnp.concatenate([x[: ROWS // 2, :HEAD_DIM], x[ROWS // 2 :, HEAD_DIM:]], axis=0)


def attend_kernel(
    length_ref, lat_hbm, code_hbm, table_hbm, scale_hbm, q_hbm, nk_hbm, nv_hbm, kf_hbm,
    mine_ref, send_ref,
    lat_buf, code_buf, table_buf, scale_buf, q_buf, nk_buf, nv_buf, kf_buf,
    lat_sem, code_sem, table_sem, small_sem,
    qc, wt, scale_rows, peak, total, numer, scores,
):
    f32, bf16 = jnp.float32, jnp.bfloat16
    kv_at = lax.axis_index("kv")
    valid = jnp.clip(length_ref[0] - kv_at * CTX_DEV, 0, CTX_DEV)
    chunks = lax.div(valid + (CHUNK - 1), CHUNK)

    small = [
        pltpu.make_async_copy(src, dst, small_sem.at[i])
        for i, (src, dst) in enumerate(
            ((kf_hbm, kf_buf), (q_hbm, q_buf), (nk_hbm, nk_buf), (nv_hbm, nv_buf), (scale_hbm, scale_buf))
        )
    ]
    for copy in small:
        copy.start()

    def at(c):
        return pl.ds(pl.multiple_of(c * CHUNK, CHUNK), CHUNK)

    def key_copies(c):
        return (
            pltpu.make_async_copy(lat_hbm.at[:, at(c)], lat_buf.at[:, at(c)], lat_sem.at[c]),
            pltpu.make_async_copy(table_hbm.at[kv_at, :, :, at(c)], table_buf.at[:, :, at(c)], table_sem.at[c]),
        )

    def code_copy(c):
        return pltpu.make_async_copy(code_hbm.at[at(c)], code_buf.at[at(c)], code_sem.at[c])

    @pl.loop(0, chunks)
    def _(c):
        for copy in key_copies(c):
            copy.start()

    @pl.loop(0, chunks)
    def _(c):
        code_copy(c).start()

    for copy in small:
        copy.wait()
    scales = scale_buf[...].astype(f32)
    for b in range(CTX_DEV // BLK):
        scale_rows[b] = jnp.broadcast_to(scales[:, b : b + 1], (KV_HEADS, HEAD_DIM))
    row_tok = lax.rem(lax.broadcasted_iota(jnp.int32, (ROWS, HEAD_DIM), 0), Q_TOK)
    lane = lax.broadcasted_iota(jnp.int32, (ROWS, HEAD_DIM), 1)
    causal = jnp.logical_and(lane <= row_tok, kv_at == 0)
    queries = q_buf[...].astype(f32)
    new_keys = nk_buf[...].astype(f32)
    new_values = nv_buf[...].astype(f32)
    pad = jnp.zeros((HEAD_DIM - Q_TOK, 2 * HEAD_DIM), f32)
    groups = HEADS // KV_HEADS
    blank = jnp.zeros((ROWS // 2, HEAD_DIM), f32)

    def head_rows(k):
        return jnp.concatenate(
            [queries[:, (k * groups + g) * HEAD_DIM : (k * groups + g + 1) * HEAD_DIM] for g in range(groups)],
            axis=0,
        )

    order = strip_order()
    source = lax.broadcasted_iota(jnp.int32, (2 * HEAD_DIM, 2 * HEAD_DIM), 0)
    target = lax.broadcasted_iota(jnp.int32, (2 * HEAD_DIM, 2 * HEAD_DIM), 1)
    strip, inside = lax.div(target, STRIP), lax.rem(target, STRIP)
    wanted = (
        lax.rem(lax.div(strip, 2), 2) * HEAD_DIM + lax.rem(strip, 2) * HALF + lax.div(strip, 4) * STRIP + inside
    )
    arrange = jnp.where(source == wanted, 1.0, 0.0).astype(bf16)

    for j in range(PAIRS):
        columns = slice(2 * j * HEAD_DIM, (2 * j + 2) * HEAD_DIM)
        plain = jnp.concatenate(
            [
                jnp.concatenate([head_rows(2 * j), blank], axis=1),
                jnp.concatenate([blank, head_rows(2 * j + 1)], axis=1),
            ],
            axis=0,
        ).astype(bf16)
        qc[j] = dot(plain, arrange).astype(bf16)
        turned = kf_buf[:, columns].astype(f32).T
        wt[columns, :] = jnp.concatenate(
            [turned[a : a + STRIP] for a in order[::STRIP]], axis=0
        ).astype(bf16)
        fresh_keys = jnp.concatenate([new_keys[:, columns], pad], axis=0).astype(bf16)
        fresh_values = jnp.concatenate([new_values[:, columns], pad], axis=0).astype(bf16)
        s = lax.dot_general(plain, fresh_keys, (((1,), (1,)), ((), ())), preferred_element_type=f32)
        s = jnp.where(causal, s, NEG_FILL)
        top = jnp.broadcast_to(jnp.max(s, axis=1, keepdims=True), s.shape)
        weights = jnp.where(causal, jnp.exp2((s - top) * EXP2_SCALE), 0.0)
        peak[j] = top
        total[j] = weights
        numer[j] = own_blocks(dot(weights.astype(bf16), fresh_values))

    def make_keys(c):
        for copy in key_copies(c):
            copy.wait()
        lat = lat_buf[:, at(c)]
        every = []
        for j in range(PAIRS):
            columns = slice(2 * j * HEAD_DIM, (2 * j + 2) * HEAD_DIM)
            cos, sin = table_buf[0, :, at(c)], table_buf[1, :, at(c)]
            pre = dot(wt[columns, :], lat)
            keys = []
            for m in range(HALF // STRIP):
                here = slice(m * STRIP, (m + 1) * STRIP)
                for i in range(2):
                    at_lo = (4 * m + 2 * i) * STRIP
                    lo, hi = pre[at_lo : at_lo + STRIP], pre[at_lo + STRIP : at_lo + 2 * STRIP]
                    keys.append((lo * cos[here] - hi * sin[here]).astype(bf16))
                    keys.append((hi * cos[here] + lo * sin[here]).astype(bf16))
            every.append(jnp.concatenate(keys, axis=0))
        return every

    def make_scores(c, keys):
        position = c * CHUNK + lax.broadcasted_iota(jnp.int32, (1, CHUNK), 1)
        hide = jnp.where(position < valid, 0.0, NEG_FILL)
        for j in range(PAIRS):
            scores[j] = dot(qc[j], keys[j]) + hide

    def weigh(j):
        s = scores[j]
        old = peak[j]
        new = jnp.maximum(old, jnp.max(s, axis=1, keepdims=True))
        shrink = jnp.exp2((old - new) * EXP2_SCALE)
        weights = [
            jnp.exp2((s[:, i : i + HEAD_DIM] - new) * EXP2_SCALE) for i in range(0, CHUNK, HEAD_DIM)
        ]
        peak[j] = new
        total[j] = total[j] * shrink + functools.reduce(jnp.add, weights)
        return shrink, [w.astype(bf16) for w in weights]

    def add_values(c, j, shrink, rounded):
        columns = slice(2 * j * HEAD_DIM, (2 * j + 2) * HEAD_DIM)
        result = numer[j] * shrink
        for b in range(CHUNK // BLK):
            per = BLK // HEAD_DIM
            w = jnp.concatenate(rounded[b * per : (b + 1) * per], axis=1)
            v = code_buf[pl.ds(pl.multiple_of(c * CHUNK + b * BLK, BLK), BLK), columns]
            part = own_blocks(dot(w, v))
            block = c * (CHUNK // BLK) + b
            factor = jnp.concatenate(
                [
                    jnp.broadcast_to(scale_rows[block, 2 * j + i : 2 * j + i + 1, :], (ROWS // 2, HEAD_DIM))
                    for i in range(2)
                ],
                axis=0,
            )
            result = result + part * factor
        numer[j] = result

    @pl.when(chunks > 0)
    def _():
        make_scores(0, make_keys(0))

    @pl.loop(0, chunks - 1)
    def _(c):
        code_copy(c).wait()
        keys = make_keys(c + 1)
        weighed = [weigh(j) for j in range(PAIRS)]
        make_scores(c + 1, keys)
        for j in range(PAIRS):
            add_values(c, j, *weighed[j])

    @pl.when(chunks > 0)
    def _():
        code_copy(chunks - 1).wait()
        weighed = [weigh(j) for j in range(PAIRS)]
        for j in range(PAIRS):
            add_values(chunks - 1, j, *weighed[j])

    for j in range(PAIRS):
        total[j] = jnp.broadcast_to(jnp.sum(total[j], axis=1, keepdims=True), (ROWS, HEAD_DIM))
    half = PAIRS // 2
    for ref, first in ((mine_ref, kv_at * half), (send_ref, (1 - kv_at) * half)):
        for part, state in enumerate((numer, peak, total)):
            for i in range(half):
                whole = state[first + i]
                for h in range(ROWS // Q_TOK):
                    column = (i * (ROWS // Q_TOK) + h) * HEAD_DIM
                    ref[part, :, column : column + HEAD_DIM] = whole[h * Q_TOK : (h + 1) * Q_TOK]


def attend(length, latents, codes, scales, queries, new_keys, new_values, key_factor):
    f32, bf16 = jnp.float32, jnp.bfloat16
    vmem = pl.BlockSpec(memory_space=pltpu.VMEM)
    hbm = pl.BlockSpec(memory_space=pltpu.HBM)
    shape = jax.ShapeDtypeStruct((3, Q_TOK, HEADS // 2 * HEAD_DIM), f32)
    macs = CTX_DEV * (RANK * KV_HEADS + 2 * PAIRS * ROWS * 2) * HEAD_DIM
    width = KV_HEADS * HEAD_DIM
    return pl.pallas_call(
        attend_kernel,
        out_shape=(shape, shape),
        in_specs=[pl.BlockSpec(memory_space=pltpu.SMEM)] + [hbm] * 8,
        out_specs=(vmem, vmem),
        scratch_shapes=[
            pltpu.VMEM((RANK, CTX_DEV), bf16),
            pltpu.VMEM((CTX_DEV, width), bf16),
            pltpu.VMEM((2, HALF, CTX_DEV), f32),
            pltpu.VMEM((KV_HEADS, CTX_DEV // BLK), bf16),
            pltpu.VMEM((Q_TOK, HEADS * HEAD_DIM), bf16),
            pltpu.VMEM((Q_TOK, width), bf16),
            pltpu.VMEM((Q_TOK, width), bf16),
            pltpu.VMEM((RANK, width), bf16),
            pltpu.SemaphoreType.DMA((N_CHUNKS,)),
            pltpu.SemaphoreType.DMA((N_CHUNKS,)),
            pltpu.SemaphoreType.DMA((N_CHUNKS,)),
            pltpu.SemaphoreType.DMA((5,)),
            pltpu.VMEM((PAIRS, ROWS, 2 * HEAD_DIM), bf16),
            pltpu.VMEM((width, RANK), bf16),
            pltpu.VMEM((CTX_DEV // BLK, KV_HEADS, HEAD_DIM), f32),
            pltpu.VMEM((PAIRS, ROWS, HEAD_DIM), f32),
            pltpu.VMEM((PAIRS, ROWS, HEAD_DIM), f32),
            pltpu.VMEM((PAIRS, ROWS, HEAD_DIM), f32),
            pltpu.VMEM((PAIRS, ROWS, CHUNK), f32),
        ],
        compiler_params=pltpu.CompilerParams(vmem_limit_bytes=36 * 2**20),
        cost_estimate=pl.CostEstimate(
            flops=2 * macs, bytes_accessed=12 * 2**20, transcendentals=CTX_DEV * HEADS * Q_TOK
        ),
        name="attend",
    )(length, *[
        pltpu.with_memory_space_constraint(x, pltpu.HBM)
        for x in (latents.T, codes, jnp.asarray(rotary_table()), scales.T, queries, new_keys, new_values, key_factor)
    ])


def merge(a, b):
    top = jnp.maximum(a[1], b[1])
    weight_a, weight_b = (jnp.exp2((x[1] - top) * EXP2_SCALE) for x in (a, b))
    numer = a[0] * weight_a + b[0] * weight_b
    return (numer / (a[2] * weight_a + b[2] * weight_b)).astype(jnp.bfloat16)


def other_core(x):
    return lax.ppermute(x, "kv", [(0, 1), (1, 0)])


AXES = {"z": 16, "y": 4, "x": 1}
SIDE = 4
WEIGHT_AXIS = ("y", "z")
FIRST_AXIS = ("z", "x")
SECOND_AXIS = ("x", "y")
SHIFTS = (1, -1, 2)
FIRST_SHIFTS = SECOND_SHIFTS = OUT_SHIFTS = (2, 1, -1)


def coordinate(chip, axis):
    return chip // AXES[axis] % SIDE


def shifted(x, axes, shift):
    moves = []
    for chip in range(SIDE**3):
        for core, axis in enumerate(axes):
            at = coordinate(chip, axis)
            target = chip + ((at + shift) % SIDE - at) * AXES[axis]
            moves.append((chip * 2 + core, target * 2 + core))
    return lax.ppermute(x, ("group", "kv"), moves)


def gathered(x, axes):
    return jnp.concatenate([x] + [shifted(x, axes, shift) for shift in SHIFTS], axis=0)


def assemble_kernel(*refs):
    *pieces, out_ref, whole = refs
    chip, core = lax.axis_index("group"), lax.axis_index("kv")

    def place(axes, at_core, shift):
        value = jnp.int32(0)
        for c, axis in enumerate(axes):
            at = lax.rem(lax.div(chip, AXES[axis]) + (shift + SIDE), SIDE) * AXES[axis]
            value = jnp.where(at_core == c, at, value)
        return value

    for at_core, refs in ((core, pieces[:SIDE]), (1 - core, pieces[SIDE:])):
        for ref, d in zip(refs, (0,) + OUT_SHIFTS):
            for i, e in enumerate((0,) + SECOND_SHIFTS):
                for j, f in enumerate((0,) + FIRST_SHIFTS):
                    request = (
                        place(WEIGHT_AXIS, at_core, d)
                        + place(FIRST_AXIS, at_core, -f)
                        + place(SECOND_AXIS, at_core, -e)
                    )
                    row = (i * SIDE + j) * Q_TOK
                    at = pl.ds(pl.multiple_of(request * Q_TOK, Q_TOK), Q_TOK)
                    block = ref[row : row + Q_TOK, :]
                    whole[at, :] = block if at_core is core else whole[at, :] + block
    half = out_ref.shape[0]
    out_ref[...] = whole[pl.ds(pl.multiple_of(core * half, half), half), :]


def assemble(own, other):
    vmem = pl.BlockSpec(memory_space=pltpu.VMEM)
    rows, columns = SIDE * own[0].shape[0], own[0].shape[1]
    return pl.pallas_call(
        assemble_kernel,
        out_shape=jax.ShapeDtypeStruct((rows // 2, columns), jnp.float32),
        in_specs=[vmem] * 8,
        out_specs=vmem,
        scratch_shapes=[pltpu.VMEM((rows, columns), jnp.float32)],
        compiler_params=pltpu.CompilerParams(vmem_limit_bytes=4 * 2**20),
        name="assemble",
    )(*own, *other)


def body(lengths, latents, codes, scales, queries, new_keys, new_values, key_factor, out_weight):
    cut = out_weight.shape[0] // 16
    before, after = (shifted(out_weight, WEIGHT_AXIS, shift) for shift in SHIFTS[:2])
    mine, send = attend(
        lengths, latents[0], codes[0], scales[0], queries[0], new_keys[0], new_values[0], key_factor
    )
    attended = merge(mine, [other_core(part) for part in send])
    before, after = lax.optimization_barrier((before, after))
    half = out_weight.shape[0] // 2
    far = [
        shifted(before[:cut], WEIGHT_AXIS, 1),
        shifted(after[cut:half], WEIGHT_AXIS, -1),
        shifted(before[half:], WEIGHT_AXIS, 1),
    ]
    blocks = [attended[None]] + [shifted(attended[None], FIRST_AXIS, shift) for shift in FIRST_SHIFTS]
    blocks[1], far[0] = lax.optimization_barrier((blocks[1], far[0]))
    near = jnp.concatenate(blocks, axis=0)
    rows = jnp.concatenate([near] + [shifted(near, SECOND_AXIS, shift) for shift in SECOND_SHIFTS], axis=0)
    rows = rows.reshape(SIDE * SIDE * Q_TOK, HEADS // 2 * HEAD_DIM)
    distant = dot(rows[:, :cut], far[0]) + dot(rows[:, cut:half], far[1]) + dot(rows[:, half:], far[2])
    distant = shifted(distant.astype(jnp.bfloat16), WEIGHT_AXIS, -2)
    pieces = [shifted(dot(rows, w).astype(jnp.bfloat16), WEIGHT_AXIS, -shift) for w, shift in zip((before, after), SHIFTS)]
    pieces = [dot(rows, out_weight)] + [p.astype(jnp.float32) for p in (distant, *pieces)]
    return assemble(pieces, [other_core(p) for p in pieces])


def solution(mesh):
    placed = (
        P("group"),
        P("group", "kv", None),
        P("group", "kv", None),
        P("group", "kv", None),
        P("group", None, None),
        P("group", None, None),
        P("group", None, None),
        P(),
        P("kv", "group"),
    )
    return jax.shard_map(
        body, mesh=mesh, in_specs=placed, out_specs=P("kv", "group"), check_vma=False
    )
```
